768 devices in a mesh: grp: 96 (over x, z, core), feat: 8 (over y).
Axes of the slice: x: 4, y: 8, z: 12, core: 2. Of those that a mesh axis runs over, the one named last changes fastest.
Arguments:
- feature_table: bfloat16 [196608, 4096], P(('grp', 'feat')), may hold values from -6 to 6
- sample_ids: int32 [98304], P(('grp', 'feat')), may hold values from 0 to 255
- block_ids: int32 [768, 4], P('grp'), may hold values from 0 to 7, as said below
- block_counts: int32 [768], P('grp'), may hold values from 1 to 4, as said below
- block_tiles: bfloat16 [768, 4, 128, 128], P('grp'), may hold values from 0.049804688 to 1
- weight: bfloat16 [4096, 1024], P('feat'), may hold values from -0.09375 to 0.09375
- target: bfloat16 [98304, 1024], P(('grp', 'feat')), may hold values from -6 to 6
Outputs:
- embedding: bfloat16 [98304, 1024], P(('grp', 'feat'))
- weight_grad: float32 [4096, 1024], P('feat')
The draws below stay inside these ranges and needn't reach their ends.
Inputs may be any that keep to these rules, and one draw needn't show every extreme that they name: `block_ids`: each row's 4 entries are distinct block numbers within the row block's group. `block_counts`: in every group some row block has all 4 slots live.
All inputs are finite; a program needn't handle non-finite values.
Results may differ from the reference program's by a relative error of at most 0.019.
Values may be sent and summed in bfloat16 or wider, within the bound.
No kernel may reach another device: no remote copies, remote signals or barrier semaphores. Data moves between devices by JAX's collectives and lax.ppermute only.
A program may use at most 32 MiB of HBM per device.

```python
import jax
import jax.numpy as jnp
from jax import lax

F = 4096
H = 1024
BLK = 128
MAXB = 4
NODE_DEV = 128
TABLE_DEV = 256
NODES = 1024
BLOCKS = 8
GRP_BLOCKS = 768
ALL_NODES = 98304
ALL_ROWS = 196608
N_GRP = 96
N_FEAT = 8


def draw_block_ids(key, part):
    key = jax.random.fold_in(key, 5)
    row_keys = jax.random.split(key, GRP_BLOCKS)
    chosen = jax.vmap(lambda row_key: jax.random.permutation(row_key, BLOCKS)[:MAXB])(row_keys)
    return chosen.astype(jnp.int32)


def draw_block_counts(key, part):
    key = jax.random.fold_in(key, 7)
    first_key, second_key, third_key = jax.random.split(key, 3)
    group_total = GRP_BLOCKS // BLOCKS
    base_counts = jax.random.randint(first_key, (group_total, BLOCKS), 1, 3)
    heavy_group = jax.random.randint(second_key, (group_total, 1), 0, 8) == 0
    counts = jnp.where(heavy_group, MAXB, base_counts)
    chosen = jax.random.randint(third_key, (group_total, 1), 0, BLOCKS)
    counts = jnp.where(jnp.arange(BLOCKS)[None, :] == chosen, MAXB, counts)
    return counts.reshape(GRP_BLOCKS).astype(jnp.int32)


def plant(entries, own_key, low, largest):
    longest = entries.shape.index(max(entries.shape))
    spots = []
    for shift in (0, 1):
        where = [jax.random.randint(jax.random.fold_in(own_key, axis), (), 0, length) for axis, length in enumerate(entries.shape)]
        where[longest] = (where[longest] + shift) % entries.shape[longest]
        spots.append(tuple(where))
    return entries.at[spots[0]].set(low).at[spots[1]].set(largest)


def steps_of(stream_key, shape, cuts, smallest, largest):
    loudness = 1.0
    for dim, blocks in cuts:
        draws = jax.random.uniform(jax.random.fold_in(jax.random.fold_in(stream_key, 6), dim), (blocks,), jnp.float32, smallest / len(cuts), largest / len(cuts))
        loudness = loudness * jnp.repeat(jnp.exp(draws), shape[dim] // blocks).reshape((-1,) + (1,) * (len(shape) - 1 - dim))
    return loudness


def noise(key, shape, scale, reach, cuts=(), kind=jnp.bfloat16):
    array = scale * jax.random.normal(key, shape, jnp.float32)
    if cuts:
        array = array * steps_of(key, shape, cuts, -0.22, 0.18)
    return jnp.clip(array, -reach, reach).astype(kind)


def setup_inputs(seed: int = 0) -> dict:
    key_list = jax.random.split(jax.random.key(seed), 8)
    feature_table = noise(key_list[0], (ALL_ROWS, F), 1.0, 6.0, ((0, 768),))
    sample_ids = plant(jax.random.randint(key_list[1], (ALL_NODES,), 0, TABLE_DEV), jax.random.fold_in(key_list[1], 1), 0, TABLE_DEV - 1).astype(jnp.int32)
    block_ids = draw_block_ids(jax.random.fold_in(key_list[7], 71), 0)
    block_counts = draw_block_counts(jax.random.fold_in(key_list[7], 71), 0)
    block_tiles = jnp.clip(0.049804688 + 0.9501953 * jax.random.uniform(key_list[4], (GRP_BLOCKS, MAXB, BLK, BLK), jnp.float32) ** steps_of(key_list[4], (GRP_BLOCKS, MAXB, BLK, BLK), ((0, 96),), -0.2, 0.2), 0.049804688, 1.0).astype(jnp.bfloat16)
    weight = noise(key_list[5], (F, H), F ** -0.5, 0.09375, ((0, 8),))
    target = noise(key_list[6], (ALL_NODES, H), 1.0, 6.0, ((0, 768),))
    return {"feature_table": feature_table, "sample_ids": sample_ids, "block_ids": block_ids, "block_counts": block_counts, "block_tiles": block_tiles, "weight": weight, "target": target}


def aggregate_group(features, group_ids, group_counts, group_tiles):
    blocked = features.reshape(BLOCKS, BLK, F)
    neighbor_rows = jnp.take(blocked, group_ids.astype(jnp.int32), axis=0)
    live_mask = (jnp.arange(MAXB, dtype=jnp.int32)[None, :] < group_counts.astype(jnp.int32)[:, None]).astype(jnp.float32)
    tile_values = group_tiles.astype(jnp.float32) * live_mask[:, :, None, None]
    summed = jnp.einsum('rsij,rsjf->rif', tile_values, neighbor_rows.astype(jnp.float32))
    degree = lax.optimization_barrier(jnp.sum(tile_values, axis=(1, 3)))
    return (summed / degree[:, :, None]).reshape(NODES, F).astype(jnp.bfloat16)

def group_pass(features, group_ids, group_counts, group_tiles, weight, group_target):
    aggregate = aggregate_group(features, group_ids, group_counts, group_tiles)
    slice_width = F // N_FEAT
    parts = jnp.einsum('njf,jfh->jnh', aggregate.reshape(NODES, N_FEAT, slice_width).astype(jnp.float32), weight.reshape(N_FEAT, slice_width, H).astype(jnp.float32))
    rounded = lax.optimization_barrier(parts.astype(jnp.bfloat16))
    preact = lax.optimization_barrier(jnp.sum(rounded.astype(jnp.float32), axis=0))
    sigmoid_part = jax.nn.sigmoid(preact)
    hidden = preact * sigmoid_part
    scales = lax.rsqrt(lax.optimization_barrier(jnp.mean(hidden * hidden, axis=1, keepdims=True)) + 1e-05)
    embedding = (hidden * scales).astype(jnp.bfloat16)
    cotangent = (embedding.astype(jnp.float32) - group_target.astype(jnp.float32)) / NODES
    projected = lax.optimization_barrier(jnp.sum(cotangent * hidden, axis=1, keepdims=True))
    grad_hidden = scales * cotangent - scales ** 3 / H * hidden * projected
    slope = sigmoid_part * (1.0 + preact * (1.0 - sigmoid_part))
    grad_pre = (grad_hidden * slope).astype(jnp.bfloat16)
    partial_grad = jnp.dot(aggregate.T, grad_pre, preferred_element_type=jnp.float32)
    return (embedding, partial_grad)

def reference(feature_table, sample_ids, block_ids, block_counts, block_tiles, weight, target):
    tables = feature_table.reshape(N_GRP, N_FEAT, TABLE_DEV, F)
    picks = sample_ids.astype(jnp.int32).reshape(N_GRP, N_FEAT, NODE_DEV)
    grouped_ids = block_ids.astype(jnp.int32).reshape(N_GRP, BLOCKS, MAXB)
    grouped_counts = block_counts.astype(jnp.int32).reshape(N_GRP, BLOCKS)
    grouped_tiles = block_tiles.reshape(N_GRP, BLOCKS, MAXB, BLK, BLK)
    grouped_target = target.reshape(N_GRP, NODES, H)

    def one_group(inputs):
        group_table, group_picks, group_ids, group_counts, group_tiles, group_target = inputs
        features = jax.vmap(lambda shard_rows, chosen: jnp.take(shard_rows, chosen, axis=0))(group_table, group_picks)
        features = features.reshape(NODES, F)
        return group_pass(features, group_ids, group_counts, group_tiles, weight, group_target)
    embeddings, partials = lax.map(one_group, (tables, picks, grouped_ids, grouped_counts, grouped_tiles, grouped_target))
    weight_grad = lax.optimization_barrier(jnp.sum(partials.astype(jnp.float32), axis=0))
    return (embeddings.reshape(ALL_NODES, H), weight_grad)
```

```python
import jax
import jax.numpy as jnp
from jax import lax
from jax.sharding import Mesh, PartitionSpec as P

GRP = ("x", "zo", "zi", "core")
ALL = GRP + ("feat",)


def exchange_sum(parts, axis):
    got = lax.all_to_all(parts, axis, 0, 0)
    return jnp.sum(got.astype(jnp.float32), axis=0)


def group_sum(term):
    rows, cols = term.shape
    with jax.named_scope("sum_core"):
        part = exchange_sum(term.astype(jnp.bfloat16).reshape(2, rows // 2, cols), "core")
    with jax.named_scope("sum_x"):
        part = exchange_sum(part.astype(jnp.bfloat16).reshape(4, rows // 8, cols), "x")
    with jax.named_scope("sum_zi"):
        part = exchange_sum(part.astype(jnp.bfloat16).reshape(4, rows // 32, cols), "zi")
    with jax.named_scope("sum_zo"):
        part = jnp.sum(lax.all_gather(part, "zo"), axis=0).astype(jnp.bfloat16)
    with jax.named_scope("gather_zi"):
        part = lax.all_gather(part, "zi", axis=0, tiled=True)
    with jax.named_scope("gather_x"):
        part = lax.all_gather(part, "x", axis=0, tiled=True)
    with jax.named_scope("gather_core"):
        other = lax.ppermute(part, "core", [(0, 1), (1, 0)])
        mine = lax.axis_index("core")
        both = jnp.stack([jnp.where(mine == 0, part, other), jnp.where(mine == 0, other, part)])
    return both.reshape(rows, cols).astype(jnp.float32)


def ring_gather(block):
    n = 8
    to_right = [(i, (i + 1) % n) for i in range(n)]
    to_left = [(i, (i - 1) % n) for i in range(n)]
    held = {0: block}
    for k in range(1, 5):
        held[k] = lax.ppermute(held[k - 1], "feat", to_right)
        if k < 4:
            held[n - k] = lax.ppermute(held[(n - k + 1) % n], "feat", to_left)
    return [held[k] for k in range(n)]


def shards(feature_table, sample_ids, block_ids, block_counts, block_tiles, weight, target):
    with jax.named_scope("pick"):
        picked = feature_table.at[sample_ids].get(mode="promise_in_bounds")
        slices = lax.all_to_all(picked, "feat", split_axis=1, concat_axis=0, tiled=True)
    node_total, slice_width = slices.shape
    block_total, slot_total, block_rows, block_width = block_tiles.shape
    with jax.named_scope("aggregate"):
        blocked = slices.reshape(block_total, block_rows, slice_width)
        live_mask = jnp.arange(slot_total, dtype=jnp.int32)[None, :] < block_counts[:, None]
        masked = jnp.where(live_mask[:, :, None, None], block_tiles, jnp.zeros((), jnp.bfloat16))
        neighbor_rows = blocked.at[block_ids].get(mode="promise_in_bounds")
        summed = jnp.einsum("rsij,rsjf->rif", masked, neighbor_rows, preferred_element_type=jnp.float32)
        degree = jnp.sum(masked.astype(jnp.float32), axis=(1, 3))
        aggregate = (summed / degree[:, :, None]).reshape(node_total, slice_width).astype(jnp.bfloat16)
    with jax.named_scope("preact"):
        partial = jnp.dot(aggregate, weight, preferred_element_type=jnp.float32).astype(jnp.bfloat16)
        preact = exchange_sum(partial.reshape(block_total, block_rows, -1), "feat")
    with jax.named_scope("grad"):
        sigmoid_part = jax.nn.sigmoid(preact)
        hidden = preact * sigmoid_part
        hidden_width = hidden.shape[1]
        scales = lax.rsqrt(jnp.mean(hidden * hidden, axis=1, keepdims=True) + 1e-05)
        embedding = (hidden * scales).astype(jnp.bfloat16)
        cotangent = (embedding.astype(jnp.float32) - target.astype(jnp.float32)) / node_total
        projected = jnp.sum(cotangent * hidden, axis=1, keepdims=True)
        grad_hidden = scales * cotangent - scales**3 / hidden_width * hidden * projected
        slope = sigmoid_part * (1.0 + preact * (1.0 - sigmoid_part))
        grad_pre = (grad_hidden * slope).astype(jnp.bfloat16)
    with jax.named_scope("fold"):
        order = (lax.axis_index("feat") - jnp.arange(block_total)) % block_total
        turned = aggregate.reshape(block_total, block_rows, slice_width).at[order].get(mode="promise_in_bounds")
        folded = lax.dot_general(
            turned.reshape(node_total, slice_width),
            jnp.concatenate(ring_gather(grad_pre), axis=0),
            (((0,), (0,)), ((), ())),
            preferred_element_type=jnp.float32,
        )
    weight_grad = group_sum(folded)
    return (embedding, weight_grad)


def solution(mesh):
    fine = Mesh(mesh.devices.reshape(4, 3, 4, 2, 8), ALL)
    return jax.shard_map(
        shards,
        mesh=fine,
        in_specs=(
            P(ALL, None),
            P(ALL),
            P(GRP, None),
            P(GRP),
            P(GRP, None, None, None),
            P("feat", None),
            P(ALL, None),
        ),
        out_specs=(P(ALL, None), P("feat", None)),
        check_vma=False,
    )
```

```python
import jax
import jax.numpy as jnp
from jax import lax
from jax.experimental import pallas as pl
from jax.experimental.pallas import tpu as pltpu
from jax.sharding import Mesh, PartitionSpec as P

GRP = ("x", "zo", "zi", "core")
ALL = GRP + ("feat",)
SWAP = [(0, 1), (1, 0)]


def exchange_sum(parts, axis):
    got = lax.all_to_all(parts, axis, 0, 0)
    return jnp.sum(got.astype(jnp.float32), axis=0)


def group_sum(term):
    rows, cols = term.shape
    with jax.named_scope("sum_x_zi"):
        part = exchange_sum(term.reshape(16, rows // 16, cols), ("x", "zi"))
    with jax.named_scope("sum_zo"):
        part = jnp.sum(lax.all_gather(part, "zo"), axis=0).astype(jnp.bfloat16)
    with jax.named_scope("gather_zi"):
        part = lax.all_gather(part, "zi", axis=0, tiled=True)
    with jax.named_scope("gather_x"):
        part = lax.all_gather(part, "x", axis=0, tiled=True)
    with jax.named_scope("gather_core"):
        other = lax.ppermute(part, "core", SWAP)
        first = lax.axis_index("core") == 0
        return jnp.concatenate([jnp.where(first, part, other), jnp.where(first, other, part)], axis=1).astype(jnp.float32)


def fold_kernel(me_ref, rows_ref, *refs):
    *grad_refs, out_ref = refs
    me = me_ref[0]
    total = None
    for k, grad_ref in enumerate(grad_refs):
        rows = rows_ref[lax.rem(me - k + len(grad_refs), len(grad_refs))]
        term = lax.dot_general(rows, grad_ref[...], (((0,), (0,)), ((), ())), preferred_element_type=jnp.float32)
        total = term if total is None else total + term
    out_ref[...] = total.astype(out_ref.dtype)


def fold(me, rows, grads):
    width, cols = rows.shape[2], grads[0].shape[1]
    vmem = pl.BlockSpec(memory_space=pltpu.VMEM)
    return pl.pallas_call(
        fold_kernel,
        out_shape=jax.ShapeDtypeStruct((width, cols), jnp.bfloat16),
        in_specs=[pl.BlockSpec(memory_space=pltpu.SMEM), vmem] + [vmem] * len(grads),
        out_specs=vmem,
        compiler_params=pltpu.CompilerParams(vmem_limit_bytes=32 * 2**20),
    )(me.reshape(1), rows, *grads)


def ring_gather(block):
    n = 8
    to_right = [(i, (i + 1) % n) for i in range(n)]
    to_left = [(i, (i - 1) % n) for i in range(n)]
    held = {0: block}
    for k in range(1, 5):
        held[k] = lax.ppermute(held[k - 1], "feat", to_right)
        if k < 4:
            held[n - k] = lax.ppermute(held[(n - k + 1) % n], "feat", to_left)
    return [held[k] for k in range(n)]


def shards(feature_table, sample_ids, block_ids, block_counts, block_tiles, weight, target):
    with jax.named_scope("pick"):
        picked = feature_table.at[sample_ids].get(mode="promise_in_bounds", wrap_negative_indices=False)
        slices = lax.all_to_all(picked, "feat", split_axis=1, concat_axis=0, tiled=True)
    node_total, slice_width = slices.shape
    block_total, slot_total, block_rows, block_width = block_tiles.shape
    with jax.named_scope("aggregate"):
        blocked = slices.reshape(block_total, block_rows, slice_width)
        live_mask = jnp.arange(slot_total, dtype=jnp.int32)[None, :] < block_counts[:, None]
        masked = jnp.where(live_mask[:, :, None, None], block_tiles, jnp.zeros((), jnp.bfloat16))
        neighbor_rows = blocked.at[block_ids].get(mode="promise_in_bounds", wrap_negative_indices=False)
        summed = jnp.einsum("rsij,rsjf->rif", masked, neighbor_rows, preferred_element_type=jnp.float32)
        degree = jnp.sum(masked.astype(jnp.float32), axis=(1, 3))
        aggregate = (summed / degree[:, :, None]).reshape(node_total, slice_width).astype(jnp.bfloat16)
        blocked_agg = aggregate.reshape(block_total, block_rows, slice_width)
        other_agg = lax.ppermute(blocked_agg, "core", SWAP)
    with jax.named_scope("preact"):
        partial = jnp.dot(aggregate, weight, preferred_element_type=jnp.float32).astype(jnp.bfloat16)
        preact = exchange_sum(partial.reshape(block_total, block_rows, -1), "feat")
    with jax.named_scope("grad"):
        sigmoid_part = jax.nn.sigmoid(preact)
        hidden = preact * sigmoid_part
        hidden_width = hidden.shape[1]
        scales = lax.rsqrt(jnp.mean(hidden * hidden, axis=1, keepdims=True) + 1e-05)
        embedding = (hidden * scales).astype(jnp.bfloat16)
        cotangent = (embedding.astype(jnp.float32) - target.astype(jnp.float32)) / node_total
        projected = jnp.sum(cotangent * hidden, axis=1, keepdims=True)
        grad_hidden = scales * cotangent - scales**3 / hidden_width * hidden * projected
        slope = sigmoid_part * (1.0 + preact * (1.0 - sigmoid_part))
        grad_pre = (grad_hidden * slope).astype(jnp.bfloat16)
    with jax.named_scope("swap"):
        half = hidden_width // 2
        paired = lax.all_to_all(grad_pre.reshape(block_rows, 2, half).swapaxes(0, 1), "core", 0, 0)
    with jax.named_scope("fold"):
        first = lax.axis_index("core") == 0
        rows = jnp.concatenate([jnp.where(first, blocked_agg, other_agg), jnp.where(first, other_agg, blocked_agg)], axis=1)
        folded = fold(lax.axis_index("feat"), rows, ring_gather(paired.reshape(2 * block_rows, half)))
    weight_grad = group_sum(folded)
    return (embedding, weight_grad)


def solution(mesh):
    fine = Mesh(mesh.devices.reshape(4, 3, 4, 2, 8), ALL)
    return jax.shard_map(
        shards,
        mesh=fine,
        in_specs=(
            P(ALL, None),
            P(ALL),
            P(GRP, None),
            P(GRP),
            P(GRP, None, None, None),
            P("feat", None),
            P(ALL, None),
        ),
        out_specs=(P(ALL, None), P("feat", None)),
        check_vma=False,
    )
```

```python
import jax
import jax.numpy as jnp
from jax import lax
from jax.experimental import pallas as pl
from jax.experimental.pallas import tpu as pltpu
from jax.sharding import Mesh, PartitionSpec as P

GRP = ("x", "zo", "zi", "core")
ALL = GRP + ("feat",)
SWAP = [(0, 1), (1, 0)]
TO_RIGHT = [(i, (i + 1) % 8) for i in range(8)]
TO_LEFT = [(i, (i - 1) % 8) for i in range(8)]


def exchange_sum(parts, axis):
    got = lax.all_to_all(parts, axis, 0, 0)
    return jnp.sum(got.astype(jnp.float32), axis=0)


def group_sum(term):
    rows, cols = term.shape
    with jax.named_scope("sum_x_zi"):
        part = exchange_sum(term.reshape(16, rows // 16, cols), ("x", "zi"))
    with jax.named_scope("sum_z"):
        parts = lax.all_gather(part.astype(jnp.bfloat16), ("zo", "zi"), axis=0, tiled=True)
        parts = parts.reshape(3, rows // 4, cols).astype(jnp.float32)
        part = jnp.sum(parts, axis=0).astype(jnp.bfloat16)
    with jax.named_scope("gather_x"):
        part = lax.all_gather(part, "x", axis=0, tiled=True)
    with jax.named_scope("gather_core"):
        other = lax.ppermute(part, "core", SWAP)
        first = lax.axis_index("core") == 0
        return jnp.concatenate([jnp.where(first, part, other), jnp.where(first, other, part)], axis=1).astype(jnp.float32)


def pick_kernel(ids_ref, table_ref, out_ref):
    wanted = lax.broadcasted_iota(jnp.int32, (table_ref.shape[0], ids_ref.shape[1]), 0) == ids_ref[...]
    rows = lax.dot_general(
        wanted.astype(table_ref.dtype), table_ref[...], (((0,), (0,)), ((), ())), preferred_element_type=jnp.float32
    )
    out_ref[0] = rows.astype(out_ref.dtype)


def pick(table, ids, slices):
    rows, width = table.shape[0], table.shape[1] // slices
    return pl.pallas_call(
        pick_kernel,
        grid=(slices,),
        out_shape=jax.ShapeDtypeStruct((slices, ids.shape[0], width), table.dtype),
        in_specs=[
            pl.BlockSpec((1, ids.shape[0]), lambda j: (0, 0)),
            pl.BlockSpec((rows, width), lambda j: (0, j)),
        ],
        out_specs=pl.BlockSpec((1, ids.shape[0], width), lambda j: (j, 0, 0)),
    )(ids.reshape(1, -1), table)


def aggregate_kernel(me_ref, ids_ref, counts_ref, slices_ref, tiles_ref, weight_ref, agg_ref, *refs):
    *part_refs, turned = refs
    blocks, block_rows, width = slices_ref.shape
    slots = tiles_ref.shape[1]
    ones = jnp.ones((slots * tiles_ref.shape[3], 128), jnp.bfloat16)
    for k in range(blocks):
        own = lax.rem(me_ref[0] + blocks // 2 - k + blocks, blocks)
        lhs = [
            jnp.where(s < counts_ref[own], tiles_ref[own, s], jnp.zeros((), jnp.bfloat16)) for s in range(slots)
        ]
        rhs = [slices_ref[ids_ref[own, s]] for s in range(slots)]
        lhs, rhs = jnp.concatenate(lhs, axis=1), jnp.concatenate(rhs, axis=0)
        summed = jnp.dot(lhs, rhs, preferred_element_type=jnp.float32)
        degree = jnp.dot(lhs, ones, preferred_element_type=jnp.float32)
        agg = (summed / jnp.concatenate([degree] * (width // 128), axis=1)).astype(jnp.bfloat16)
        agg_ref[own] = agg
        turned[pl.ds(k * block_rows, block_rows)] = agg
    step = 4
    for k in range(0, blocks, step):
        lhs = turned[pl.ds(k * block_rows, step * block_rows)]
        parts = jnp.dot(lhs, weight_ref[...], preferred_element_type=jnp.float32).astype(jnp.bfloat16)
        for i in range(step):
            part_refs[k + i][...] = parts[i * block_rows:(i + 1) * block_rows]


def aggregate_and_project(me, ids, counts, slices, tiles, weight):
    blocks, block_rows, width = slices.shape
    vmem, smem = pl.BlockSpec(memory_space=pltpu.VMEM), pl.BlockSpec(memory_space=pltpu.SMEM)
    part = jax.ShapeDtypeStruct((block_rows, weight.shape[1]), jnp.bfloat16)
    agg, *parts = pl.pallas_call(
        aggregate_kernel,
        out_shape=[jax.ShapeDtypeStruct(slices.shape, jnp.bfloat16)] + [part] * blocks,
        in_specs=[smem] * 3 + [vmem] * 3,
        out_specs=[vmem] * (1 + blocks),
        scratch_shapes=[pltpu.VMEM((blocks * block_rows, width), jnp.bfloat16)],
        compiler_params=pltpu.CompilerParams(vmem_limit_bytes=32 * 2**20),
    )(me.reshape(1), ids, counts, slices, tiles, weight)
    return agg, parts


def ring_sum(parts):
    right, left = parts[0], parts[7]
    for k in range(1, 5):
        right = lax.ppermute(right, "feat", TO_RIGHT).astype(jnp.float32) + parts[k].astype(jnp.float32)
        right = right.astype(jnp.bfloat16) if k < 4 else right
        if k < 4:
            left = lax.ppermute(left, "feat", TO_LEFT)
            if k < 3:
                left = (left.astype(jnp.float32) + parts[7 - k].astype(jnp.float32)).astype(jnp.bfloat16)
    return right + left.astype(jnp.float32)


def fold_kernel(me_ref, rows_ref, *refs):
    *grad_refs, out_ref = refs
    me = me_ref[0]
    total = None
    for k, grad_ref in enumerate(grad_refs):
        rows = rows_ref[lax.rem(me - k + len(grad_refs), len(grad_refs))]
        term = lax.dot_general(rows, grad_ref[...], (((0,), (0,)), ((), ())), preferred_element_type=jnp.float32)
        total = term if total is None else total + term
    out_ref[...] = total.astype(out_ref.dtype)


def fold(me, rows, grads):
    width, cols = rows.shape[2], grads[0].shape[1]
    vmem = pl.BlockSpec(memory_space=pltpu.VMEM)
    return pl.pallas_call(
        fold_kernel,
        out_shape=jax.ShapeDtypeStruct((width, cols), jnp.bfloat16),
        in_specs=[pl.BlockSpec(memory_space=pltpu.SMEM), vmem] + [vmem] * len(grads),
        out_specs=vmem,
        compiler_params=pltpu.CompilerParams(vmem_limit_bytes=32 * 2**20),
    )(me.reshape(1), rows, *grads)


def ring_gather(block):
    n = 8
    held = {0: block}
    for k in range(1, 5):
        held[k] = lax.ppermute(held[k - 1], "feat", TO_RIGHT)
        if k < 4:
            held[n - k] = lax.ppermute(held[(n - k + 1) % n], "feat", TO_LEFT)
    return [held[k] for k in range(n)]


def shards(feature_table, sample_ids, block_ids, block_counts, block_tiles, weight, target):
    block_total, slot_total, block_rows, block_width = block_tiles.shape
    node_total = block_total * block_rows
    me = lax.axis_index("feat")
    with jax.named_scope("pick"):
        slices = lax.all_to_all(pick(feature_table, sample_ids, block_total), "feat", 0, 0)
    with jax.named_scope("aggregate"):
        agg, parts = aggregate_and_project(me, block_ids, block_counts, slices, block_tiles, weight)
        other_agg = lax.ppermute(agg, "core", SWAP)
    with jax.named_scope("preact"):
        preact = ring_sum(parts)
    with jax.named_scope("grad"):
        sigmoid_part = jax.nn.sigmoid(preact)
        hidden = preact * sigmoid_part
        hidden_width = hidden.shape[1]
        scales = lax.rsqrt(jnp.mean(hidden * hidden, axis=1, keepdims=True) + 1e-05)
        embedding = (hidden * scales).astype(jnp.bfloat16)
        cotangent = (embedding.astype(jnp.float32) - target.astype(jnp.float32)) / node_total
        projected = jnp.sum(cotangent * hidden, axis=1, keepdims=True)
        grad_hidden = scales * cotangent - scales**3 / hidden_width * hidden * projected
        slope = sigmoid_part * (1.0 + preact * (1.0 - sigmoid_part))
        grad_pre = (grad_hidden * slope).astype(jnp.bfloat16)
    with jax.named_scope("swap"):
        half = hidden_width // 2
        paired = lax.all_to_all(grad_pre.reshape(block_rows, 2, half).swapaxes(0, 1), "core", 0, 0)
    with jax.named_scope("fold"):
        first = lax.axis_index("core") == 0
        rows = jnp.concatenate([jnp.where(first, agg, other_agg), jnp.where(first, other_agg, agg)], axis=1)
        folded = fold(me, rows, ring_gather(paired.reshape(2 * block_rows, half)))
    weight_grad = group_sum(folded)
    return (embedding, weight_grad)


def solution(mesh):
    fine = Mesh(mesh.devices.reshape(4, 3, 4, 2, 8), ALL)
    return jax.shard_map(
        shards,
        mesh=fine,
        in_specs=(
            P(ALL, None),
            P(ALL),
            P(GRP, None),
            P(GRP),
            P(GRP, None, None, None),
            P("feat", None),
            P(ALL, None),
        ),
        out_specs=(P(ALL, None), P("feat", None)),
        check_vma=False,
    )
```

```python
import jax
import jax.numpy as jnp
from jax import lax
from jax.experimental import pallas as pl
from jax.experimental.pallas import tpu as pltpu
from jax.sharding import Mesh, PartitionSpec as P

GRP = ("x", "zo", "zi", "core")
ALL = GRP + ("feat",)
SWAP = [(0, 1), (1, 0)]
FEAT = 8
CORE_FEAT = ("core", "feat")


def ring_step(ahead):
    pairs = []
    for i in range(FEAT):
        pairs.append((i, (i + ahead) % FEAT))
        pairs.append((FEAT + i, FEAT + (i - ahead) % FEAT))
    return pairs


FORTH, BACK = ring_step(1), ring_step(-1)


def turn():
    return 1 - 2 * lax.axis_index("core")


def exchange_sum(parts, axis):
    got = lax.all_to_all(parts, axis, 0, 0)
    return jnp.sum(got.astype(jnp.float32), axis=0)


def group_sum(term):
    rows, cols = term.shape
    with jax.named_scope("sum_x_zi"):
        part = exchange_sum(term.reshape(16, rows // 16, cols), ("x", "zi"))
    with jax.named_scope("sum_z"):
        parts = lax.all_gather(part.astype(jnp.bfloat16), ("zo", "zi"), axis=0, tiled=True)
        parts = parts.reshape(3, rows // 4, cols).astype(jnp.float32)
        part = jnp.sum(parts, axis=0).astype(jnp.bfloat16)
    with jax.named_scope("gather_x"):
        part = lax.all_gather(part, "x", axis=0, tiled=True)
    with jax.named_scope("gather_core"):
        other = lax.ppermute(part, "core", SWAP)
        first = lax.axis_index("core") == 0
        return jnp.concatenate([jnp.where(first, part, other), jnp.where(first, other, part)], axis=1).astype(jnp.float32)


def pick_kernel(ids_ref, table_ref, out_ref):
    slices, _, width = out_ref.shape
    wanted = lax.broadcasted_iota(jnp.int32, (table_ref.shape[0], ids_ref.shape[1]), 0) == ids_ref[...]
    wanted = wanted.astype(jnp.float32).T.astype(table_ref.dtype)
    for j in range(slices):
        rows = jnp.dot(wanted, table_ref[:, j * width:(j + 1) * width], preferred_element_type=jnp.float32)
        out_ref[j] = rows.astype(out_ref.dtype)


def pick(table, ids, slices):
    vmem = pl.BlockSpec(memory_space=pltpu.VMEM)
    return pl.pallas_call(
        pick_kernel,
        out_shape=jax.ShapeDtypeStruct((slices, ids.shape[0], table.shape[1] // slices), table.dtype),
        in_specs=[vmem, vmem],
        out_specs=vmem,
        compiler_params=pltpu.CompilerParams(vmem_limit_bytes=32 * 2**20),
    )(ids.reshape(1, -1), table)


def aggregate_kernel(place_ref, ids_ref, counts_ref, slices_ref, tiles_ref, weight_ref, agg_ref, *refs):
    *part_refs, turned = refs
    blocks, block_rows, width = slices_ref.shape
    slots = tiles_ref.shape[1]
    ones = jnp.ones((slots * tiles_ref.shape[3], 128), jnp.bfloat16)
    for k in range(blocks):
        own = lax.rem(place_ref[0] + place_ref[1] * (blocks // 2 - k) + blocks, blocks)
        lhs = [
            jnp.where(s < counts_ref[own], tiles_ref[own, s], jnp.zeros((), jnp.bfloat16)) for s in range(slots)
        ]
        rhs = [slices_ref[ids_ref[own, s]] for s in range(slots)]
        lhs, rhs = jnp.concatenate(lhs, axis=1), jnp.concatenate(rhs, axis=0)
        summed = jnp.dot(lhs, rhs, preferred_element_type=jnp.float32)
        degree = jnp.dot(lhs, ones, preferred_element_type=jnp.float32)
        agg = (summed / jnp.concatenate([degree] * (width // 128), axis=1)).astype(jnp.bfloat16)
        agg_ref[own] = agg
        turned[pl.ds(k * block_rows, block_rows)] = agg
    step = 4
    for k in range(0, blocks, step):
        lhs = turned[pl.ds(k * block_rows, step * block_rows)]
        parts = jnp.dot(lhs, weight_ref[...], preferred_element_type=jnp.float32).astype(jnp.bfloat16)
        for i in range(step):
            part_refs[k + i][...] = parts[i * block_rows:(i + 1) * block_rows]


def aggregate_and_project(place, ids, counts, slices, tiles, weight):
    blocks, block_rows, width = slices.shape
    vmem, smem = pl.BlockSpec(memory_space=pltpu.VMEM), pl.BlockSpec(memory_space=pltpu.SMEM)
    part = jax.ShapeDtypeStruct((block_rows, weight.shape[1]), jnp.bfloat16)
    agg, *parts = pl.pallas_call(
        aggregate_kernel,
        out_shape=[jax.ShapeDtypeStruct(slices.shape, jnp.bfloat16)] + [part] * blocks,
        in_specs=[smem] * 3 + [vmem] * 3,
        out_specs=[vmem] * (1 + blocks),
        scratch_shapes=[pltpu.VMEM((blocks * block_rows, width), jnp.bfloat16)],
        compiler_params=pltpu.CompilerParams(vmem_limit_bytes=32 * 2**20),
    )(place, ids, counts, slices, tiles, weight)
    return agg, parts


def ring_sum(parts):
    forth, back = parts[0], parts[7]
    for k in range(1, 5):
        forth = lax.ppermute(forth, CORE_FEAT, FORTH).astype(jnp.float32) + parts[k].astype(jnp.float32)
        forth = forth.astype(jnp.bfloat16) if k < 4 else forth
        if k < 4:
            back = lax.ppermute(back, CORE_FEAT, BACK)
            if k < 3:
                back = (back.astype(jnp.float32) + parts[7 - k].astype(jnp.float32)).astype(jnp.bfloat16)
    return forth + back.astype(jnp.float32)


def ring_gather(block):
    held = {0: block}
    for k in range(1, 5):
        held[k] = lax.ppermute(held[k - 1], CORE_FEAT, FORTH)
        if k < 4:
            held[FEAT - k] = lax.ppermute(held[(FEAT - k + 1) % FEAT], CORE_FEAT, BACK)
    return [held[k] for k in range(FEAT)]


def fold_kernel(place_ref, rows_ref, *refs):
    *grad_refs, out_ref = refs
    me, turned = place_ref[0], place_ref[1]
    total = None
    for k, grad_ref in enumerate(grad_refs):
        rows = rows_ref[lax.rem(me - turned * k + len(grad_refs), len(grad_refs))]
        term = lax.dot_general(rows, grad_ref[...], (((0,), (0,)), ((), ())), preferred_element_type=jnp.float32)
        total = term if total is None else total + term
    out_ref[...] = total.astype(out_ref.dtype)


def fold(place, rows, grads):
    width, cols = rows.shape[2], grads[0].shape[1]
    vmem = pl.BlockSpec(memory_space=pltpu.VMEM)
    return pl.pallas_call(
        fold_kernel,
        out_shape=jax.ShapeDtypeStruct((width, cols), jnp.bfloat16),
        in_specs=[pl.BlockSpec(memory_space=pltpu.SMEM), vmem] + [vmem] * len(grads),
        out_specs=vmem,
        compiler_params=pltpu.CompilerParams(vmem_limit_bytes=32 * 2**20),
    )(place, rows, *grads)


def shards(feature_table, sample_ids, block_ids, block_counts, block_tiles, weight, target):
    block_total, slot_total, block_rows, block_width = block_tiles.shape
    node_total = block_total * block_rows
    place = jnp.stack([lax.axis_index("feat"), turn()])
    with jax.named_scope("pick"):
        slices = lax.all_to_all(pick(feature_table, sample_ids, block_total), "feat", 0, 0)
    with jax.named_scope("aggregate"):
        agg, parts = aggregate_and_project(place, block_ids, block_counts, slices, block_tiles, weight)
        other_agg = lax.ppermute(agg, "core", SWAP)
    with jax.named_scope("preact"):
        preact = ring_sum(parts)
    with jax.named_scope("grad"):
        sigmoid_part = jax.nn.sigmoid(preact)
        hidden = preact * sigmoid_part
        hidden_width = hidden.shape[1]
        scales = lax.rsqrt(jnp.mean(hidden * hidden, axis=1, keepdims=True) + 1e-05)
        embedding = (hidden * scales).astype(jnp.bfloat16)
        cotangent = (embedding.astype(jnp.float32) - target.astype(jnp.float32)) / node_total
        projected = jnp.sum(cotangent * hidden, axis=1, keepdims=True)
        grad_hidden = scales * cotangent - scales**3 / hidden_width * hidden * projected
        slope = sigmoid_part * (1.0 + preact * (1.0 - sigmoid_part))
        grad_pre = (grad_hidden * slope).astype(jnp.bfloat16)
    with jax.named_scope("swap"):
        half = hidden_width // 2
        paired = lax.all_to_all(grad_pre.reshape(block_rows, 2, half).swapaxes(0, 1), "core", 0, 0)
    with jax.named_scope("fold"):
        first = lax.axis_index("core") == 0
        rows = jnp.concatenate([jnp.where(first, agg, other_agg), jnp.where(first, other_agg, agg)], axis=1)
        folded = fold(place, rows, ring_gather(paired.reshape(2 * block_rows, half)))
    weight_grad = group_sum(folded)
    return (embedding, weight_grad)


def solution(mesh):
    fine = Mesh(mesh.devices.reshape(4, 3, 4, 2, 8), ALL)
    return jax.shard_map(
        shards,
        mesh=fine,
        in_specs=(
            P(ALL, None),
            P(ALL),
            P(GRP, None),
            P(GRP),
            P(GRP, None, None, None),
            P("feat", None),
            P(ALL, None),
        ),
        out_specs=(P(ALL, None), P("feat", None)),
        check_vma=False,
    )
```

```python
import jax
import jax.numpy as jnp
from jax import lax
from jax.experimental import pallas as pl
from jax.experimental.pallas import tpu as pltpu
from jax.sharding import Mesh, PartitionSpec as P

GRP = ("x", "zo", "zi", "core")
ALL = GRP + ("feat",)
SWAP = [(0, 1), (1, 0)]
FEAT = 8


def neighbours(chain, odd_step):
    first = (chain + odd_step) % 2
    pairs = [((i + first) % FEAT, (i + 1 + first) % FEAT) for i in range(0, FEAT, 2)]
    return pairs + [(j, i) for i, j in pairs]


def with_neighbour(block, chain, odd_step):
    return lax.ppermute(block, "feat", neighbours(chain, odd_step))


def is_second(chain):
    return (lax.axis_index("feat") + chain) % 2 == 1


def exchange_sum(parts, axis):
    got = lax.all_to_all(parts, axis, 0, 0)
    return jnp.sum(got.astype(jnp.float32), axis=0)


def group_sum(term):
    rows, cols = term.shape
    with jax.named_scope("sum_x_zi"):
        part = exchange_sum(term.reshape(16, rows // 16, cols), ("x", "zi"))
    with jax.named_scope("sum_z"):
        parts = lax.all_gather(part.astype(jnp.bfloat16), ("zo", "zi"), axis=0, tiled=True)
        parts = parts.reshape(3, rows // 4, cols).astype(jnp.float32)
        part = jnp.sum(parts, axis=0).astype(jnp.bfloat16)
    with jax.named_scope("gather_x"):
        part = lax.all_gather(part, "x", axis=0, tiled=True)
    with jax.named_scope("gather_core"):
        other = lax.ppermute(part, "core", SWAP)
        first = lax.axis_index("core") == 0
        return jnp.concatenate([jnp.where(first, part, other), jnp.where(first, other, part)], axis=1).astype(jnp.float32)


def pick_kernel(ids_ref, table_ref, out_ref):
    slices, _, width = out_ref.shape
    wanted = lax.broadcasted_iota(jnp.int32, (table_ref.shape[0], ids_ref.shape[1]), 0) == ids_ref[...]
    wanted = wanted.astype(jnp.float32).T.astype(table_ref.dtype)
    for j in range(slices):
        rows = jnp.dot(wanted, table_ref[:, j * width:(j + 1) * width], preferred_element_type=jnp.float32)
        out_ref[j] = rows.astype(out_ref.dtype)


def pick(table, ids, slices):
    vmem = pl.BlockSpec(memory_space=pltpu.VMEM)
    return pl.pallas_call(
        pick_kernel,
        out_shape=jax.ShapeDtypeStruct((slices, ids.shape[0], table.shape[1] // slices), table.dtype),
        in_specs=[vmem, vmem],
        out_specs=vmem,
        compiler_params=pltpu.CompilerParams(vmem_limit_bytes=32 * 2**20),
    )(ids.reshape(1, -1), table)


def pair_block(me, chain, k, member):
    rank = lax.rem(me + chain, FEAT)
    side = 2 * lax.rem(rank, 2) - 1
    pair = lax.div(rank, 2) + (0, side, -side, 2)[k] + FEAT // 2
    return lax.rem(2 * lax.rem(pair, FEAT // 2) + member + FEAT - chain, FEAT)


def aggregate_kernel(me_ref, ids_ref, counts_ref, slices_ref, tiles_ref, weight_ref, agg_ref, *part_refs):
    blocks, _, width = slices_ref.shape
    slots = tiles_ref.shape[1]
    ones = jnp.ones((slots * tiles_ref.shape[3], 128), jnp.bfloat16)
    for own in range(blocks):
        lhs = [
            jnp.where(s < counts_ref[own], tiles_ref[own, s], jnp.zeros((), jnp.bfloat16)) for s in range(slots)
        ]
        rhs = [slices_ref[ids_ref[own, s]] for s in range(slots)]
        lhs, rhs = jnp.concatenate(lhs, axis=1), jnp.concatenate(rhs, axis=0)
        summed = jnp.dot(lhs, rhs, preferred_element_type=jnp.float32)
        degree = jnp.dot(lhs, ones, preferred_element_type=jnp.float32)
        agg_ref[own] = (summed / jnp.concatenate([degree] * (width // 128), axis=1)).astype(jnp.bfloat16)
    for chain in range(2):
        refs = part_refs[4 * chain:4 * chain + 4]
        cols = refs[0].shape[2]
        order = [(k, member) for k in (3, 2, 1, 0) for member in range(2)]
        lhs = jnp.concatenate([agg_ref[pair_block(me_ref[0], chain, k, member)] for k, member in order], axis=0)
        parts = jnp.dot(lhs, weight_ref[:, chain * cols:(chain + 1) * cols], preferred_element_type=jnp.float32)
        parts = parts.astype(jnp.bfloat16)
        rows = parts.shape[0] // blocks
        for i, (k, member) in enumerate(order):
            refs[k][member] = parts[i * rows:(i + 1) * rows]


def aggregate_and_project(me, ids, counts, slices, tiles, weight):
    block_rows = slices.shape[1]
    vmem, smem = pl.BlockSpec(memory_space=pltpu.VMEM), pl.BlockSpec(memory_space=pltpu.SMEM)
    pair = jax.ShapeDtypeStruct((2, block_rows, weight.shape[1] // 2), jnp.bfloat16)
    agg, *parts = pl.pallas_call(
        aggregate_kernel,
        out_shape=[jax.ShapeDtypeStruct(slices.shape, jnp.bfloat16)] + [pair] * 8,
        in_specs=[smem] * 3 + [vmem] * 3,
        out_specs=[vmem] * 9,
        compiler_params=pltpu.CompilerParams(vmem_limit_bytes=32 * 2**20),
    )(me.reshape(1), ids, counts, slices, tiles, weight)
    return agg, (parts[:4], parts[4:])


def add(a, b):
    return a.astype(jnp.float32) + b.astype(jnp.float32)


def chain_sum(pairs):
    held = [pairs[chain][3] for chain in range(2)]
    for k in (2, 1):
        got = [with_neighbour(held[chain], chain, (k + 1) % 2) for chain in range(2)]
        held = [add(got[chain], pairs[chain][k]).astype(jnp.bfloat16) for chain in range(2)]
    sums = []
    got = [with_neighbour(held[chain], chain, 1) for chain in range(2)]
    both = [add(got[chain], pairs[chain][0]) for chain in range(2)]
    for chain in range(2):
        second = is_second(chain)
        give = jnp.where(second, both[chain][0], both[chain][1]).astype(jnp.bfloat16)
        keep = jnp.where(second, both[chain][1], both[chain][0])
        sums.append(keep + with_neighbour(give, chain, 0).astype(jnp.float32))
    return jnp.concatenate(sums, axis=1)


def chain_gather(blocks):
    got = [with_neighbour(blocks[chain], chain, 0) for chain in range(2)]
    held = []
    for chain in range(2):
        second = is_second(chain)
        mine, other = blocks[chain], got[chain]
        held.append([jnp.stack([jnp.where(second, other, mine), jnp.where(second, mine, other)])])
    for k in range(1, 4):
        for chain in range(2):
            held[chain].append(with_neighbour(held[chain][-1], chain, k % 2))
    return held[0] + held[1]


def fold_kernel(me_ref, rows_ref, *refs):
    *grad_refs, out_ref = refs
    for chain in range(2):
        cols = grad_refs[0].shape[2]
        total = None
        for k in range(4):
            for member in range(2):
                rows = rows_ref[pair_block(me_ref[0], chain, k, member)]
                term = lax.dot_general(
                    rows, grad_refs[4 * chain + k][member], (((0,), (0,)), ((), ())), preferred_element_type=jnp.float32
                )
                total = term if total is None else total + term
        out_ref[:, chain * cols:(chain + 1) * cols] = total.astype(out_ref.dtype)


def fold(me, rows, grads):
    vmem = pl.BlockSpec(memory_space=pltpu.VMEM)
    return pl.pallas_call(
        fold_kernel,
        out_shape=jax.ShapeDtypeStruct((rows.shape[2], 2 * grads[0].shape[2]), jnp.bfloat16),
        in_specs=[pl.BlockSpec(memory_space=pltpu.SMEM), vmem] + [vmem] * len(grads),
        out_specs=vmem,
        compiler_params=pltpu.CompilerParams(vmem_limit_bytes=32 * 2**20),
    )(me.reshape(1), rows, *grads)


def shards(feature_table, sample_ids, block_ids, block_counts, block_tiles, weight, target):
    block_total, slot_total, block_rows, block_width = block_tiles.shape
    node_total = block_total * block_rows
    me = lax.axis_index("feat")
    with jax.named_scope("pick"):
        slices = lax.all_to_all(pick(feature_table, sample_ids, block_total), "feat", 0, 0)
    with jax.named_scope("aggregate"):
        agg, parts = aggregate_and_project(me, block_ids, block_counts, slices, block_tiles, weight)
        other_agg = lax.ppermute(agg, "core", SWAP)
    with jax.named_scope("preact"):
        preact = chain_sum(parts)
    with jax.named_scope("grad"):
        sigmoid_part = jax.nn.sigmoid(preact)
        hidden = preact * sigmoid_part
        hidden_width = hidden.shape[1]
        scales = lax.rsqrt(jnp.mean(hidden * hidden, axis=1, keepdims=True) + 1e-05)
        embedding = (hidden * scales).astype(jnp.bfloat16)
        cotangent = (embedding.astype(jnp.float32) - target.astype(jnp.float32)) / node_total
        projected = jnp.sum(cotangent * hidden, axis=1, keepdims=True)
        grad_hidden = scales * cotangent - scales**3 / hidden_width * hidden * projected
        slope = sigmoid_part * (1.0 + preact * (1.0 - sigmoid_part))
        grad_pre = (grad_hidden * slope).astype(jnp.bfloat16)
    with jax.named_scope("swap"):
        half = hidden_width // 2
        paired = lax.all_to_all(grad_pre.reshape(block_rows, 2, half).swapaxes(0, 1), "core", 0, 0)
    with jax.named_scope("fold"):
        first = lax.axis_index("core") == 0
        rows = jnp.concatenate([jnp.where(first, agg, other_agg), jnp.where(first, other_agg, agg)], axis=1)
        paired = paired.reshape(2 * block_rows, half)
        folded = fold(me, rows, chain_gather([paired[:, :half // 2], paired[:, half // 2:]]))
    weight_grad = group_sum(folded)
    return (embedding, weight_grad)


def solution(mesh):
    fine = Mesh(mesh.devices.reshape(4, 3, 4, 2, 8), ALL)
    return jax.shard_map(
        shards,
        mesh=fine,
        in_specs=(
            P(ALL, None),
            P(ALL),
            P(GRP, None),
            P(GRP),
            P(GRP, None, None, None),
            P("feat", None),
            P(ALL, None),
        ),
        out_specs=(P(ALL, None), P("feat", None)),
        check_vma=False,
    )
```

```python
import jax
import jax.numpy as jnp
from jax import lax
from jax.experimental import pallas as pl
from jax.experimental.pallas import tpu as pltpu
from jax.sharding import Mesh, PartitionSpec as P

GRP = ("x", "zo", "zi", "core")
ALL = GRP + ("feat",)
SWAP = [(0, 1), (1, 0)]
FEAT = 8


def neighbours(chain, odd_step):
    first = (chain + odd_step) % 2
    pairs = [((i + first) % FEAT, (i + 1 + first) % FEAT) for i in range(0, FEAT, 2)]
    return pairs + [(j, i) for i, j in pairs]


def with_neighbour(block, chain, odd_step):
    return lax.ppermute(block, "feat", neighbours(chain, odd_step))


def is_second(chain):
    return (lax.axis_index("feat") + chain) % 2 == 1


def exchange_sum(parts, axis):
    got = lax.all_to_all(parts, axis, 0, 0)
    return jnp.sum(got.astype(jnp.float32), axis=0)


def group_sum(term):
    rows, cols = term.shape
    with jax.named_scope("sum_x_zi"):
        part = exchange_sum(term.reshape(16, rows // 16, cols), ("x", "zi"))
    with jax.named_scope("sum_z"):
        parts = lax.all_gather(part.astype(jnp.bfloat16), ("zo", "zi"), axis=0, tiled=True)
        parts = parts.reshape(3, rows // 4, cols).astype(jnp.float32)
        part = jnp.sum(parts, axis=0).astype(jnp.bfloat16)
    with jax.named_scope("gather_x"):
        part = lax.all_gather(part, "x", axis=0, tiled=True)
    with jax.named_scope("gather_core"):
        other = lax.ppermute(part, "core", SWAP)
        first = lax.axis_index("core") == 0
        return jnp.concatenate([jnp.where(first, part, other), jnp.where(first, other, part)], axis=1).astype(jnp.float32)


def pick_kernel(ids_ref, table_ref, out_ref, ids, table, ids_sem, sems):
    slices, _, width = out_ref.shape
    copies = [pltpu.make_async_copy(ids_ref, ids, ids_sem)]
    for j in range(slices):
        cols = pl.ds(j * width, width)
        copies.append(pltpu.make_async_copy(table_ref.at[:, cols], table.at[:, cols], sems.at[j]))
    for copy in copies:
        copy.start()
    copies[0].wait()
    wanted = lax.broadcasted_iota(jnp.int32, (table.shape[0], ids.shape[1]), 0) == ids[...]
    wanted = wanted.astype(jnp.float32).T.astype(table.dtype)
    for j in range(slices):
        copies[j + 1].wait()
        rows = jnp.dot(wanted, table[:, j * width:(j + 1) * width], preferred_element_type=jnp.float32)
        out_ref[j] = rows.astype(out_ref.dtype)


def pick(table, ids, slices):
    hbm = pl.BlockSpec(memory_space=pltpu.HBM)
    ids = ids.reshape(1, -1)
    return pl.pallas_call(
        pick_kernel,
        out_shape=jax.ShapeDtypeStruct((slices, ids.shape[1], table.shape[1] // slices), table.dtype),
        in_specs=[hbm, hbm],
        out_specs=pl.BlockSpec(memory_space=pltpu.VMEM),
        scratch_shapes=[
            pltpu.VMEM(ids.shape, ids.dtype),
            pltpu.VMEM(table.shape, table.dtype),
            pltpu.SemaphoreType.DMA,
            pltpu.SemaphoreType.DMA((slices,)),
        ],
        compiler_params=pltpu.CompilerParams(vmem_limit_bytes=60 * 2**20),
    )(ids, table)


def pair_block(me, chain, k, member):
    rank = lax.rem(me + chain, FEAT)
    side = 2 * lax.rem(rank, 2) - 1
    pair = lax.div(rank, 2) + (0, side, -side, 2)[k] + FEAT // 2
    return lax.rem(2 * lax.rem(pair, FEAT // 2) + member + FEAT - chain, FEAT)


def aggregate_kernel(me_ref, ids_ref, counts_ref, slices_ref, tiles_ref, weight_ref, agg_ref, *part_refs):
    blocks, _, width = slices_ref.shape
    slots = tiles_ref.shape[1]
    ones = jnp.ones((slots * tiles_ref.shape[3], 128), jnp.bfloat16)
    for own in range(blocks):
        lhs = [
            jnp.where(s < counts_ref[own], tiles_ref[own, s], jnp.zeros((), jnp.bfloat16)) for s in range(slots)
        ]
        rhs = [slices_ref[ids_ref[own, s]] for s in range(slots)]
        lhs, rhs = jnp.concatenate(lhs, axis=1), jnp.concatenate(rhs, axis=0)
        summed = jnp.dot(lhs, rhs, preferred_element_type=jnp.float32)
        degree = jnp.dot(lhs, ones, preferred_element_type=jnp.float32)
        agg_ref[own] = (summed / jnp.concatenate([degree] * (width // 128), axis=1)).astype(jnp.bfloat16)
    for chain in range(2):
        refs = part_refs[4 * chain:4 * chain + 4]
        cols = refs[0].shape[2]
        order = [(k, member) for k in (3, 2, 1, 0) for member in range(2)]
        lhs = jnp.concatenate([agg_ref[pair_block(me_ref[0], chain, k, member)] for k, member in order], axis=0)
        parts = jnp.dot(lhs, weight_ref[:, chain * cols:(chain + 1) * cols], preferred_element_type=jnp.float32)
        parts = parts.astype(jnp.bfloat16)
        rows = parts.shape[0] // blocks
        for i, (k, member) in enumerate(order):
            refs[k][member] = parts[i * rows:(i + 1) * rows]


def aggregate_and_project(me, ids, counts, slices, tiles, weight):
    block_rows = slices.shape[1]
    vmem, smem = pl.BlockSpec(memory_space=pltpu.VMEM), pl.BlockSpec(memory_space=pltpu.SMEM)
    pair = jax.ShapeDtypeStruct((2, block_rows, weight.shape[1] // 2), jnp.bfloat16)
    agg, *parts = pl.pallas_call(
        aggregate_kernel,
        out_shape=[jax.ShapeDtypeStruct(slices.shape, jnp.bfloat16)] + [pair] * 8,
        in_specs=[smem] * 3 + [vmem] * 3,
        out_specs=[vmem] * 9,
        compiler_params=pltpu.CompilerParams(vmem_limit_bytes=16 * 2**20),
    )(me.reshape(1), ids, counts, slices, tiles, weight)
    return agg, (parts[:4], parts[4:])


def add(a, b):
    return a.astype(jnp.float32) + b.astype(jnp.float32)


def chain_sum(pairs):
    held = [pairs[chain][3] for chain in range(2)]
    for k in (2, 1):
        got = [with_neighbour(held[chain], chain, (k + 1) % 2) for chain in range(2)]
        held = [add(got[chain], pairs[chain][k]).astype(jnp.bfloat16) for chain in range(2)]
    sums = []
    got = [with_neighbour(held[chain], chain, 1) for chain in range(2)]
    for chain in range(2):
        second = is_second(chain)
        give, keep = (
            add(jnp.where(second, x[0], x[1]), jnp.where(second, y[0], y[1]))
            for x, y in ((got[chain], pairs[chain][0]), (got[chain][::-1], pairs[chain][0][::-1]))
        )
        sums.append(keep + with_neighbour(give.astype(jnp.bfloat16), chain, 0).astype(jnp.float32))
    return jnp.concatenate(sums, axis=1)


def chain_gather(blocks):
    got = [with_neighbour(blocks[chain], chain, 0) for chain in range(2)]
    held = []
    for chain in range(2):
        second = is_second(chain)
        mine, other = blocks[chain], got[chain]
        held.append([jnp.stack([jnp.where(second, other, mine), jnp.where(second, mine, other)])])
    for k in range(1, 4):
        for chain in range(2):
            held[chain].append(with_neighbour(held[chain][-1], chain, k % 2))
    return held[0] + held[1]


def fold_kernel(me_ref, agg_ref, other_ref, *refs):
    *grad_refs, out_ref = refs
    for chain in range(2):
        cols = grad_refs[0].shape[2]
        total = None
        for k in range(4):
            for member in range(2):
                block = pair_block(me_ref[0], chain, k, member)
                rows = jnp.concatenate([agg_ref[block], other_ref[block]], axis=0)
                term = lax.dot_general(
                    rows, grad_refs[4 * chain + k][member], (((0,), (0,)), ((), ())), preferred_element_type=jnp.float32
                )
                total = term if total is None else total + term
        out_ref[:, chain * cols:(chain + 1) * cols] = total.astype(out_ref.dtype)


def fold(me, agg, other_agg, grads):
    vmem = pl.BlockSpec(memory_space=pltpu.VMEM)
    return pl.pallas_call(
        fold_kernel,
        out_shape=jax.ShapeDtypeStruct((agg.shape[2], 2 * grads[0].shape[2]), jnp.bfloat16),
        in_specs=[pl.BlockSpec(memory_space=pltpu.SMEM)] + [vmem] * (2 + len(grads)),
        out_specs=vmem,
        compiler_params=pltpu.CompilerParams(vmem_limit_bytes=12 * 2**20),
    )(me.reshape(1), agg, other_agg, *grads)


def shards(feature_table, sample_ids, block_ids, block_counts, block_tiles, weight, target):
    block_total, slot_total, block_rows, block_width = block_tiles.shape
    node_total = block_total * block_rows
    me = lax.axis_index("feat")
    with jax.named_scope("pick"):
        slices = lax.all_to_all(pick(feature_table, sample_ids, block_total), "feat", 0, 0)
    with jax.named_scope("aggregate"):
        agg, parts = aggregate_and_project(me, block_ids, block_counts, slices, block_tiles, weight)
        other_agg = lax.ppermute(agg, "core", SWAP)
    with jax.named_scope("preact"):
        preact = chain_sum(parts)
    with jax.named_scope("grad"):
        sigmoid_part = jax.nn.sigmoid(preact)
        hidden = preact * sigmoid_part
        hidden_width = hidden.shape[1]
        scales = lax.rsqrt(jnp.mean(hidden * hidden, axis=1, keepdims=True) + 1e-05)
        embedding = (hidden * scales).astype(jnp.bfloat16)
        cotangent = (embedding.astype(jnp.float32) - target.astype(jnp.float32)) / node_total
        projected = jnp.sum(cotangent * hidden, axis=1, keepdims=True)
        grad_hidden = scales * cotangent - scales**3 / hidden_width * hidden * projected
        slope = sigmoid_part * (1.0 + preact * (1.0 - sigmoid_part))
        grad_pre = (grad_hidden * slope).astype(jnp.bfloat16)
    with jax.named_scope("swap"):
        half = hidden_width // 2
        first = lax.axis_index("core") == 0
        left, right = grad_pre[:, :half], grad_pre[:, half:]
        mine, other = jnp.where(first, left, right), lax.ppermute(jnp.where(first, right, left), "core", SWAP)
        paired = jnp.concatenate([mine, other], axis=0)
    with jax.named_scope("fold"):
        folded = fold(me, agg, other_agg, chain_gather([paired[:, :half // 2], paired[:, half // 2:]]))
    weight_grad = group_sum(folded)
    return (embedding, weight_grad)


def solution(mesh):
    fine = Mesh(mesh.devices.reshape(4, 3, 4, 2, 8), ALL)
    return jax.shard_map(
        shards,
        mesh=fine,
        in_specs=(
            P(ALL, None),
            P(ALL),
            P(GRP, None),
            P(GRP),
            P(GRP, None, None, None),
            P("feat", None),
            P(ALL, None),
        ),
        out_specs=(P(ALL, None), P("feat", None)),
        check_vma=False,
    )
```

```python
import jax
import jax.numpy as jnp
from jax import lax
from jax.experimental import pallas as pl
from jax.experimental.pallas import tpu as pltpu
from jax.sharding import Mesh, PartitionSpec as P

GRP = ("x", "zo", "zi", "core")
ALL = GRP + ("feat",)
SWAP = [(0, 1), (1, 0)]
FEAT = 8


def neighbours(chain, odd_step):
    first = (chain + odd_step) % 2
    pairs = [((i + first) % FEAT, (i + 1 + first) % FEAT) for i in range(0, FEAT, 2)]
    return pairs + [(j, i) for i, j in pairs]


def with_neighbour(block, chain, odd_step):
    return lax.ppermute(block, "feat", neighbours(chain, odd_step))


def is_second(chain):
    return (lax.axis_index("feat") + chain) % 2 == 1


def exchange_sum(parts, axis):
    got = lax.all_to_all(parts, axis, 0, 0)
    return jnp.sum(got.astype(jnp.float32), axis=0)


def group_sum(term):
    rows, cols = term.shape
    with jax.named_scope("sum_x_zi"):
        part = exchange_sum(term.reshape(16, rows // 16, cols), ("x", "zi"))
    with jax.named_scope("sum_z"):
        parts = lax.all_gather(part.astype(jnp.bfloat16), ("zo", "zi"), axis=0, tiled=True)
        parts = parts.reshape(3, rows // 4, cols).astype(jnp.float32)
        part = jnp.sum(parts, axis=0).astype(jnp.bfloat16)
    with jax.named_scope("gather_x"):
        part = lax.all_gather(part, "x", axis=0, tiled=True)
    with jax.named_scope("gather_core"):
        other = lax.ppermute(part, "core", SWAP)
        first = lax.axis_index("core") == 0
        return jnp.concatenate([jnp.where(first, part, other), jnp.where(first, other, part)], axis=1).astype(jnp.float32)


def pick_kernel(ids_ref, table_ref, out_ref, ids, table, picked, ids_sem, sems, out_sems):
    slices, _, width = out_ref.shape
    copies = [pltpu.make_async_copy(ids_ref, ids, ids_sem)]
    for j in range(slices):
        cols = pl.ds(j * width, width)
        copies.append(pltpu.make_async_copy(table_ref.at[:, cols], table.at[:, cols], sems.at[j]))
    for copy in copies:
        copy.start()
    copies[0].wait()
    wanted = lax.broadcasted_iota(jnp.int32, (table.shape[0], ids.shape[1]), 0) == ids[...]
    wanted = wanted.astype(jnp.float32).T.astype(table.dtype)
    leave = []
    for j in range(slices):
        copies[j + 1].wait()
        rows = jnp.dot(wanted, table[:, j * width:(j + 1) * width], preferred_element_type=jnp.float32)
        picked[j] = rows.astype(picked.dtype)
        leave.append(pltpu.make_async_copy(picked.at[j], out_ref.at[j], out_sems.at[j]))
        leave[-1].start()
    for copy in leave:
        copy.wait()


def pick(table, ids, slices):
    hbm = pl.BlockSpec(memory_space=pltpu.HBM)
    ids = ids.reshape(1, -1)
    out = jax.ShapeDtypeStruct((slices, ids.shape[1], table.shape[1] // slices), table.dtype)
    return pl.pallas_call(
        pick_kernel,
        out_shape=out,
        in_specs=[hbm, hbm],
        out_specs=hbm,
        scratch_shapes=[
            pltpu.VMEM(ids.shape, ids.dtype),
            pltpu.VMEM(table.shape, table.dtype),
            pltpu.VMEM(out.shape, out.dtype),
            pltpu.SemaphoreType.DMA,
            pltpu.SemaphoreType.DMA((slices,)),
            pltpu.SemaphoreType.DMA((slices,)),
        ],
        compiler_params=pltpu.CompilerParams(vmem_limit_bytes=60 * 2**20),
    )(ids, table)


def pair_block(me, chain, k, member):
    rank = lax.rem(me + chain, FEAT)
    side = 2 * lax.rem(rank, 2) - 1
    pair = lax.div(rank, 2) + (0, side, -side, 2)[k] + FEAT // 2
    return lax.rem(2 * lax.rem(pair, FEAT // 2) + member + FEAT - chain, FEAT)


def aggregate_kernel(ids_ref, counts_ref, slices_ref, tiles_ref, agg_ref):
    blocks, _, width = slices_ref.shape
    slots = tiles_ref.shape[1]
    ones = jnp.ones((slots * tiles_ref.shape[3], 128), jnp.bfloat16)
    for own in range(blocks):
        lhs = [
            jnp.where(s < counts_ref[own], tiles_ref[own, s], jnp.zeros((), jnp.bfloat16)) for s in range(slots)
        ]
        rhs = [slices_ref[ids_ref[own, s]] for s in range(slots)]
        lhs, rhs = jnp.concatenate(lhs, axis=1), jnp.concatenate(rhs, axis=0)
        summed = jnp.dot(lhs, rhs, preferred_element_type=jnp.float32)
        degree = jnp.dot(lhs, ones, preferred_element_type=jnp.float32)
        agg_ref[own] = (summed / jnp.concatenate([degree] * (width // 128), axis=1)).astype(jnp.bfloat16)


def mean_of_blocks(ids, counts, slices, tiles):
    vmem, smem = pl.BlockSpec(memory_space=pltpu.VMEM), pl.BlockSpec(memory_space=pltpu.SMEM)
    return pl.pallas_call(
        aggregate_kernel,
        out_shape=jax.ShapeDtypeStruct(slices.shape, jnp.bfloat16),
        in_specs=[smem] * 2 + [vmem] * 2,
        out_specs=vmem,
        compiler_params=pltpu.CompilerParams(vmem_limit_bytes=16 * 2**20),
    )(ids, counts, slices, tiles)


def project_kernel(me_ref, agg_ref, weight_ref, *part_refs):
    blocks, rows, _ = agg_ref.shape
    for chain in range(2):
        refs = part_refs[4 * chain:4 * chain + 4]
        cols = refs[0].shape[2]
        order = [(k, member) for k in (3, 2, 1, 0) for member in range(2)]
        lhs = jnp.concatenate([agg_ref[pair_block(me_ref[0], chain, k, member)] for k, member in order], axis=0)
        parts = jnp.dot(lhs, weight_ref[:, chain * cols:(chain + 1) * cols], preferred_element_type=jnp.float32)
        parts = parts.astype(jnp.bfloat16)
        for i, (k, member) in enumerate(order):
            refs[k][member] = parts[i * rows:(i + 1) * rows]


def project(me, agg, weight):
    vmem = pl.BlockSpec(memory_space=pltpu.VMEM)
    pair = jax.ShapeDtypeStruct((2, agg.shape[1], weight.shape[1] // 2), jnp.bfloat16)
    parts = pl.pallas_call(
        project_kernel,
        out_shape=[pair] * 8,
        in_specs=[pl.BlockSpec(memory_space=pltpu.SMEM), vmem, vmem],
        out_specs=[vmem] * 8,
        compiler_params=pltpu.CompilerParams(vmem_limit_bytes=16 * 2**20),
    )(me.reshape(1), agg, weight)
    return parts[:4], parts[4:]


def add(a, b):
    return a.astype(jnp.float32) + b.astype(jnp.float32)


def chain_sum(pairs):
    held = [pairs[chain][3] for chain in range(2)]
    for k in (2, 1):
        got = [with_neighbour(held[chain], chain, (k + 1) % 2) for chain in range(2)]
        held = [add(got[chain], pairs[chain][k]).astype(jnp.bfloat16) for chain in range(2)]
    sums = []
    got = [with_neighbour(held[chain], chain, 1) for chain in range(2)]
    for chain in range(2):
        second = is_second(chain)
        give, keep = (
            add(jnp.where(second, x[0], x[1]), jnp.where(second, y[0], y[1]))
            for x, y in ((got[chain], pairs[chain][0]), (got[chain][::-1], pairs[chain][0][::-1]))
        )
        sums.append(keep + with_neighbour(give.astype(jnp.bfloat16), chain, 0).astype(jnp.float32))
    return jnp.concatenate(sums, axis=1)


def chain_gather(blocks):
    got = [with_neighbour(blocks[chain], chain, 0) for chain in range(2)]
    held = []
    for chain in range(2):
        second = is_second(chain)
        mine, other = blocks[chain], got[chain]
        held.append([jnp.stack([jnp.where(second, other, mine), jnp.where(second, mine, other)])])
    for k in range(1, 4):
        for chain in range(2):
            held[chain].append(with_neighbour(held[chain][-1], chain, k % 2))
    return held[0] + held[1]


def fold_kernel(me_ref, agg_ref, *refs):
    grad_refs, out_refs = refs[:8], refs[8:]
    for chain in range(2):
        total = None
        for k in range(4):
            grads = grad_refs[4 * chain + k][...]
            rows = jnp.concatenate([agg_ref[pair_block(me_ref[0], chain, k, member)] for member in range(2)], axis=0)
            term = lax.dot_general(
                rows, grads.reshape(rows.shape[0], -1), (((0,), (0,)), ((), ())), preferred_element_type=jnp.float32
            )
            total = term if total is None else total + term
        out_refs[chain][...] = total.astype(out_refs[chain].dtype)


def fold(me, agg, grads):
    vmem = pl.BlockSpec(memory_space=pltpu.VMEM)
    out = jax.ShapeDtypeStruct((agg.shape[2], grads[0].shape[2]), jnp.bfloat16)
    return pl.pallas_call(
        fold_kernel,
        out_shape=[out, out],
        in_specs=[pl.BlockSpec(memory_space=pltpu.SMEM)] + [vmem] * (1 + len(grads)),
        out_specs=[vmem, vmem],
        compiler_params=pltpu.CompilerParams(vmem_limit_bytes=16 * 2**20),
    )(me.reshape(1), agg, *grads)


def shards(feature_table, sample_ids, block_ids, block_counts, block_tiles, weight, target):
    block_total, slot_total, block_rows, block_width = block_tiles.shape
    node_total = block_total * block_rows
    me = lax.axis_index("feat")
    with jax.named_scope("pick"):
        slices = lax.all_to_all(pick(feature_table, sample_ids, block_total), "feat", 0, 0)
    with jax.named_scope("aggregate"):
        agg = mean_of_blocks(block_ids, block_counts, slices, block_tiles)
        parts = project(me, agg, weight)
    with jax.named_scope("preact"):
        preact = chain_sum(parts)
    with jax.named_scope("grad"):
        sigmoid_part = jax.nn.sigmoid(preact)
        hidden = preact * sigmoid_part
        hidden_width = hidden.shape[1]
        scales = lax.rsqrt(jnp.mean(hidden * hidden, axis=1, keepdims=True) + 1e-05)
        embedding = (hidden * scales).astype(jnp.bfloat16)
        cotangent = (embedding.astype(jnp.float32) - target.astype(jnp.float32)) / node_total
        projected = jnp.sum(cotangent * hidden, axis=1, keepdims=True)
        grad_hidden = scales * cotangent - scales**3 / hidden_width * hidden * projected
        slope = sigmoid_part * (1.0 + preact * (1.0 - sigmoid_part))
        grad_pre = (grad_hidden * slope).astype(jnp.bfloat16)
    with jax.named_scope("fold"):
        half = hidden_width // 2
        left, right = fold(me, agg, chain_gather([grad_pre[:, :half], grad_pre[:, half:]]))
    with jax.named_scope("sum_core"):
        first = lax.axis_index("core") == 0
        other = lax.ppermute(jnp.where(first, right, left), "core", SWAP)
        folded = add(jnp.where(first, left, right), other).astype(jnp.bfloat16)
    weight_grad = group_sum(folded)
    return (embedding, weight_grad)


def solution(mesh):
    fine = Mesh(mesh.devices.reshape(4, 3, 4, 2, 8), ALL)
    return jax.shard_map(
        shards,
        mesh=fine,
        in_specs=(
            P(ALL, None),
            P(ALL),
            P(GRP, None),
            P(GRP),
            P(GRP, None, None, None),
            P("feat", None),
            P(ALL, None),
        ),
        out_specs=(P(ALL, None), P("feat", None)),
        check_vma=False,
    )
```

```python
import functools

import jax
import jax.numpy as jnp
from jax import lax
from jax.experimental import pallas as pl
from jax.experimental.pallas import tpu as pltpu
from jax.sharding import Mesh, PartitionSpec as P

GRP = ("x", "zo", "zi", "core")
ALL = GRP + ("feat",)
SWAP = [(0, 1), (1, 0)]
FEAT = 8


def neighbours(chain, odd_step):
    first = (chain + odd_step) % 2
    pairs = [((i + first) % FEAT, (i + 1 + first) % FEAT) for i in range(0, FEAT, 2)]
    return pairs + [(j, i) for i, j in pairs]


def with_neighbour(block, chain, odd_step):
    return lax.ppermute(block, "feat", neighbours(chain, odd_step))


def is_second(chain):
    return (lax.axis_index("feat") + chain) % 2 == 1


def exchange_sum(parts, axis):
    got = lax.all_to_all(parts, axis, 0, 0)
    return jnp.sum(got.astype(jnp.float32), axis=0)


def group_sum(term):
    rows, cols = term.shape
    with jax.named_scope("sum_x_zi"):
        part = exchange_sum(term.reshape(16, rows // 16, cols), ("x", "zi"))
    with jax.named_scope("sum_z"):
        parts = lax.all_gather(part.astype(jnp.bfloat16), ("zo", "zi"), axis=0, tiled=True)
        parts = parts.reshape(3, rows // 4, cols).astype(jnp.float32)
        part = jnp.sum(parts, axis=0).astype(jnp.bfloat16)
    with jax.named_scope("gather_x"):
        part = lax.all_gather(part, "x", axis=0, tiled=True)
    with jax.named_scope("gather_core"):
        other = lax.ppermute(part, "core", SWAP)
        first = lax.axis_index("core") == 0
        return jnp.concatenate([jnp.where(first, part, other), jnp.where(first, other, part)], axis=1).astype(jnp.float32)


def pick_kernel(ids_ref, table_ref, out_ref):
    slices, _, width = out_ref.shape
    wanted = lax.broadcasted_iota(jnp.int32, (table_ref.shape[0], ids_ref.shape[1]), 0) == ids_ref[...]
    wanted = wanted.astype(jnp.float32).T.astype(table_ref.dtype)
    for j in range(slices):
        rows = jnp.dot(wanted, table_ref[:, j * width:(j + 1) * width], preferred_element_type=jnp.float32)
        out_ref[j] = rows.astype(out_ref.dtype)


def pick(table, ids, slices):
    vmem = pl.BlockSpec(memory_space=pltpu.VMEM)
    return pl.pallas_call(
        pick_kernel,
        out_shape=jax.ShapeDtypeStruct((slices, ids.shape[0], table.shape[1] // slices), table.dtype),
        in_specs=[vmem, vmem],
        out_specs=vmem,
        compiler_params=pltpu.CompilerParams(vmem_limit_bytes=16 * 2**20),
    )(ids.reshape(1, -1), table)


def pair_block(me, chain, k, member):
    rank = lax.rem(me + chain, FEAT)
    side = 2 * lax.rem(rank, 2) - 1
    pair = lax.div(rank, 2) + (0, side, -side, 2)[k] + FEAT // 2
    return lax.rem(2 * lax.rem(pair, FEAT // 2) + member + FEAT - chain, FEAT)


def aggregate_kernel(me_ref, ids_ref, counts_ref, slices_ref, tiles_ref, weight_ref, agg_ref, *part_refs):
    blocks, _, width = slices_ref.shape
    slots = tiles_ref.shape[1]
    ones = jnp.ones((slots * tiles_ref.shape[3], 128), jnp.bfloat16)
    for own in range(blocks):
        lhs = [
            jnp.where(s < counts_ref[own], tiles_ref[own, s], jnp.zeros((), jnp.bfloat16)) for s in range(slots)
        ]
        rhs = [slices_ref[ids_ref[own, s]] for s in range(slots)]
        lhs, rhs = jnp.concatenate(lhs, axis=1), jnp.concatenate(rhs, axis=0)
        summed = jnp.dot(lhs, rhs, preferred_element_type=jnp.float32)
        degree = jnp.dot(lhs, ones, preferred_element_type=jnp.float32)
        agg_ref[own] = (summed / jnp.concatenate([degree] * (width // 128), axis=1)).astype(jnp.bfloat16)
    project_kernel((3,), me_ref, agg_ref, weight_ref, *part_refs)


def aggregate(me, ids, counts, slices, tiles, weight):
    vmem, smem = pl.BlockSpec(memory_space=pltpu.VMEM), pl.BlockSpec(memory_space=pltpu.SMEM)
    pair = jax.ShapeDtypeStruct((2, slices.shape[1], weight.shape[1] // 2), jnp.bfloat16)
    return pl.pallas_call(
        aggregate_kernel,
        out_shape=[jax.ShapeDtypeStruct(slices.shape, jnp.bfloat16), pair, pair],
        in_specs=[smem] * 3 + [vmem] * 3,
        out_specs=[vmem] * 3,
        compiler_params=pltpu.CompilerParams(vmem_limit_bytes=16 * 2**20),
    )(me.reshape(1), ids, counts, slices, tiles, weight)


def project_kernel(wanted, me_ref, agg_ref, weight_ref, *part_refs):
    rows = agg_ref.shape[1]
    count = len(wanted)
    for chain in range(2):
        refs = part_refs[count * chain:count * (chain + 1)]
        cols = refs[0].shape[2]
        blocks = [pair_block(me_ref[0], chain, k, member) for k in wanted for member in range(2)]
        lhs = jnp.concatenate([agg_ref[block] for block in blocks], axis=0)
        parts = jnp.dot(lhs, weight_ref[:, chain * cols:(chain + 1) * cols], preferred_element_type=jnp.float32)
        parts = parts.astype(jnp.bfloat16)
        for i in range(2 * count):
            refs[i // 2][i % 2] = parts[i * rows:(i + 1) * rows]


def project(wanted, me, agg, weight):
    vmem = pl.BlockSpec(memory_space=pltpu.VMEM)
    pair = jax.ShapeDtypeStruct((2, agg.shape[1], weight.shape[1] // 2), jnp.bfloat16)
    count = len(wanted)
    parts = pl.pallas_call(
        functools.partial(project_kernel, wanted),
        out_shape=[pair] * (2 * count),
        in_specs=[pl.BlockSpec(memory_space=pltpu.SMEM), vmem, vmem],
        out_specs=[vmem] * (2 * count),
        compiler_params=pltpu.CompilerParams(vmem_limit_bytes=16 * 2**20),
    )(me.reshape(1), agg, weight)
    return parts[:count], parts[count:]


def add(a, b):
    return a.astype(jnp.float32) + b.astype(jnp.float32)


def chain_sum(pairs):
    held = [pairs[chain][3] for chain in range(2)]
    for k in (2, 1):
        got = [with_neighbour(held[chain], chain, (k + 1) % 2) for chain in range(2)]
        held = [add(got[chain], pairs[chain][k]).astype(jnp.bfloat16) for chain in range(2)]
    sums = []
    got = [with_neighbour(held[chain], chain, 1) for chain in range(2)]
    for chain in range(2):
        second = is_second(chain)
        give, keep = (
            add(jnp.where(second, x[0], x[1]), jnp.where(second, y[0], y[1]))
            for x, y in ((got[chain], pairs[chain][0]), (got[chain][::-1], pairs[chain][0][::-1]))
        )
        sums.append(keep + with_neighbour(give.astype(jnp.bfloat16), chain, 0).astype(jnp.float32))
    return jnp.concatenate(sums, axis=1)


def chain_gather(blocks):
    got = [with_neighbour(blocks[chain], chain, 0) for chain in range(2)]
    held = []
    for chain in range(2):
        second = is_second(chain)
        mine, other = blocks[chain], got[chain]
        held.append([jnp.stack([jnp.where(second, other, mine), jnp.where(second, mine, other)])])
    for k in range(1, 4):
        for chain in range(2):
            held[chain].append(with_neighbour(held[chain][-1], chain, k % 2))
    return held


def fold_kernel(wanted, started, me_ref, agg_ref, other_ref, *refs):
    count = len(wanted)
    grad_refs, out_ref = refs[started:started + 2 * count], refs[-1]
    for chain in range(2):
        cols = grad_refs[0].shape[2]
        place = (slice(None), slice(chain * cols, (chain + 1) * cols))
        total = refs[0][place] if started else None
        for i, k in enumerate(wanted):
            for member in range(2):
                block = pair_block(me_ref[0], chain, k, member)
                rows = jnp.concatenate([agg_ref[block], other_ref[block]], axis=0)
                term = lax.dot_general(
                    rows, grad_refs[count * chain + i][member], (((0,), (0,)), ((), ())), preferred_element_type=jnp.float32
                )
                total = term if total is None else total + term
        out_ref[place] = total.astype(out_ref.dtype)


def fold(wanted, me, agg, other_agg, grads, start, kind):
    vmem = pl.BlockSpec(memory_space=pltpu.VMEM)
    grads = [*start, *(chain[k] for chain in grads for k in wanted)]
    return pl.pallas_call(
        functools.partial(fold_kernel, wanted, len(start)),
        out_shape=jax.ShapeDtypeStruct((agg.shape[2], 2 * grads[-1].shape[2]), kind),
        in_specs=[pl.BlockSpec(memory_space=pltpu.SMEM)] + [vmem] * (2 + len(grads)),
        out_specs=vmem,
        compiler_params=pltpu.CompilerParams(vmem_limit_bytes=16 * 2**20),
    )(me.reshape(1), agg, other_agg, *grads)


def shards(feature_table, sample_ids, block_ids, block_counts, block_tiles, weight, target):
    block_total, slot_total, block_rows, block_width = block_tiles.shape
    node_total = block_total * block_rows
    me = lax.axis_index("feat")
    with jax.named_scope("pick"):
        slices = lax.all_to_all(pick(feature_table, sample_ids, block_total), "feat", 0, 0)
    with jax.named_scope("aggregate"):
        agg, *far = aggregate(me, block_ids, block_counts, slices, block_tiles, weight)
        other_agg = lax.ppermute(agg, "core", SWAP)
        near = project((0, 1, 2), me, agg, weight)
        parts = [[*near[chain], far[chain]] for chain in range(2)]
    with jax.named_scope("preact"):
        preact, other_agg = lax.optimization_barrier((chain_sum(parts), other_agg))
    with jax.named_scope("grad"):
        sigmoid_part = jax.nn.sigmoid(preact)
        hidden = preact * sigmoid_part
        hidden_width = hidden.shape[1]
        scales = lax.rsqrt(jnp.mean(hidden * hidden, axis=1, keepdims=True) + 1e-05)
        embedding = (hidden * scales).astype(jnp.bfloat16)
        cotangent = (embedding.astype(jnp.float32) - target.astype(jnp.float32)) / node_total
        projected = jnp.sum(cotangent * hidden, axis=1, keepdims=True)
        grad_hidden = scales * cotangent - scales**3 / hidden_width * hidden * projected
        slope = sigmoid_part * (1.0 + preact * (1.0 - sigmoid_part))
        grad_pre = (grad_hidden * slope).astype(jnp.bfloat16)
    with jax.named_scope("swap"):
        half = hidden_width // 2
        first = lax.axis_index("core") == 0
        left, right = grad_pre[:, :half], grad_pre[:, half:]
        mine, other = jnp.where(first, left, right), lax.ppermute(jnp.where(first, right, left), "core", SWAP)
        paired = jnp.concatenate([mine, other], axis=0)
    with jax.named_scope("fold"):
        grads = chain_gather([paired[:, :half // 2], paired[:, half // 2:]])
        folded = fold((0, 1, 2), me, agg, other_agg, grads, [], jnp.float32)
        folded = fold((3,), me, agg, other_agg, grads, [folded], jnp.bfloat16)
    weight_grad = group_sum(folded)
    return (embedding, weight_grad)


def solution(mesh):
    fine = Mesh(mesh.devices.reshape(4, 3, 4, 2, 8), ALL)
    return jax.shard_map(
        shards,
        mesh=fine,
        in_specs=(
            P(ALL, None),
            P(ALL),
            P(GRP, None),
            P(GRP),
            P(GRP, None, None, None),
            P("feat", None),
            P(ALL, None),
        ),
        out_specs=(P(ALL, None), P("feat", None)),
        check_vma=False,
    )
```

```python
import functools

import jax
import jax.numpy as jnp
from jax import lax
from jax.experimental import pallas as pl
from jax.experimental.pallas import tpu as pltpu
from jax.sharding import Mesh, PartitionSpec as P

GRP = ("x", "zo", "zi", "core")
ALL = GRP + ("feat",)
SWAP = [(0, 1), (1, 0)]
FEAT = 8


def neighbours(chain, odd_step):
    first = (chain + odd_step) % 2
    pairs = [((i + first) % FEAT, (i + 1 + first) % FEAT) for i in range(0, FEAT, 2)]
    return pairs + [(j, i) for i, j in pairs]


def with_neighbour(block, chain, odd_step):
    return lax.ppermute(block, "feat", neighbours(chain, odd_step))


def is_second(chain):
    return (lax.axis_index("feat") + chain) % 2 == 1


def exchange_sum(parts, axis):
    got = lax.all_to_all(parts, axis, 0, 0)
    return jnp.sum(got.astype(jnp.float32), axis=0)


def group_sum(term):
    rows, cols = term.shape
    with jax.named_scope("sum_x_zi"):
        part = exchange_sum(term.reshape(16, rows // 16, cols), ("x", "zi"))
    with jax.named_scope("sum_z"):
        parts = lax.all_gather(part.astype(jnp.bfloat16), ("zo", "zi"), axis=0, tiled=True)
        parts = parts.reshape(3, rows // 4, cols).astype(jnp.float32)
        part = jnp.sum(parts, axis=0).astype(jnp.bfloat16)
    with jax.named_scope("gather_x"):
        part = lax.all_gather(part, "x", axis=0, tiled=True)
    with jax.named_scope("gather_core"):
        other = lax.ppermute(part, "core", SWAP)
        first = lax.axis_index("core") == 0
        return jnp.concatenate([jnp.where(first, part, other), jnp.where(first, other, part)], axis=1).astype(jnp.float32)


def pick_kernel(wanted_ref, table_ref, out_ref):
    slices, _, width = out_ref.shape
    wanted = wanted_ref[...].T.astype(table_ref.dtype)
    for j in range(slices):
        rows = jnp.dot(wanted, table_ref[:, j * width:(j + 1) * width], preferred_element_type=jnp.float32)
        out_ref[j] = rows.astype(out_ref.dtype)


def pick(table, ids, slices):
    vmem = pl.BlockSpec(memory_space=pltpu.VMEM)
    shape = (table.shape[0], ids.shape[0])
    wanted = (lax.broadcasted_iota(jnp.int32, shape, 0) == ids[None, :]).astype(jnp.float32)
    return pl.pallas_call(
        pick_kernel,
        out_shape=jax.ShapeDtypeStruct((slices, ids.shape[0], table.shape[1] // slices), table.dtype),
        in_specs=[vmem, vmem],
        out_specs=vmem,
        compiler_params=pltpu.CompilerParams(vmem_limit_bytes=16 * 2**20),
    )(wanted, table)


def pair_block(me, chain, k, member):
    rank = lax.rem(me + chain, FEAT)
    side = 2 * lax.rem(rank, 2) - 1
    pair = lax.div(rank, 2) + (0, side, -side, 2)[k] + FEAT // 2
    return lax.rem(2 * lax.rem(pair, FEAT // 2) + member + FEAT - chain, FEAT)


def aggregate_kernel(me_ref, ids_ref, counts_ref, slices_ref, tiles_ref, weight_ref, agg_ref, *part_refs):
    blocks, _, width = slices_ref.shape
    slots = tiles_ref.shape[1]
    ones = jnp.ones((slots * tiles_ref.shape[3], 128), jnp.bfloat16)
    for own in range(blocks):
        lhs = [
            jnp.where(s < counts_ref[own], tiles_ref[own, s], jnp.zeros((), jnp.bfloat16)) for s in range(slots)
        ]
        rhs = [slices_ref[ids_ref[own, s]] for s in range(slots)]
        lhs, rhs = jnp.concatenate(lhs, axis=1), jnp.concatenate(rhs, axis=0)
        summed = jnp.dot(lhs, rhs, preferred_element_type=jnp.float32)
        degree = jnp.dot(lhs, ones, preferred_element_type=jnp.float32)
        agg_ref[own] = (summed / jnp.concatenate([degree] * (width // 128), axis=1)).astype(jnp.bfloat16)
    project_kernel((3,), me_ref, agg_ref, weight_ref, *part_refs)


def aggregate(me, ids, counts, slices, tiles, weight):
    vmem, smem = pl.BlockSpec(memory_space=pltpu.VMEM), pl.BlockSpec(memory_space=pltpu.SMEM)
    pair = jax.ShapeDtypeStruct((2, slices.shape[1], weight.shape[1] // 2), jnp.bfloat16)
    return pl.pallas_call(
        aggregate_kernel,
        out_shape=[jax.ShapeDtypeStruct(slices.shape, jnp.bfloat16), pair, pair],
        in_specs=[smem] * 3 + [vmem] * 3,
        out_specs=[vmem] * 3,
        compiler_params=pltpu.CompilerParams(vmem_limit_bytes=16 * 2**20),
    )(me.reshape(1), ids, counts, slices, tiles, weight)


def project_kernel(wanted, me_ref, agg_ref, weight_ref, *part_refs):
    rows = agg_ref.shape[1]
    count = len(wanted)
    for chain in range(2):
        refs = part_refs[count * chain:count * (chain + 1)]
        cols = refs[0].shape[2]
        blocks = [pair_block(me_ref[0], chain, k, member) for k in wanted for member in range(2)]
        lhs = jnp.concatenate([agg_ref[block] for block in blocks], axis=0)
        parts = jnp.dot(lhs, weight_ref[:, chain * cols:(chain + 1) * cols], preferred_element_type=jnp.float32)
        parts = parts.astype(jnp.bfloat16)
        for i in range(2 * count):
            refs[i // 2][i % 2] = parts[i * rows:(i + 1) * rows]


def project(wanted, me, agg, weight):
    vmem = pl.BlockSpec(memory_space=pltpu.VMEM)
    pair = jax.ShapeDtypeStruct((2, agg.shape[1], weight.shape[1] // 2), jnp.bfloat16)
    count = len(wanted)
    parts = pl.pallas_call(
        functools.partial(project_kernel, wanted),
        out_shape=[pair] * (2 * count),
        in_specs=[pl.BlockSpec(memory_space=pltpu.SMEM), vmem, vmem],
        out_specs=[vmem] * (2 * count),
        compiler_params=pltpu.CompilerParams(vmem_limit_bytes=16 * 2**20),
    )(me.reshape(1), agg, weight)
    return parts[:count], parts[count:]


def add(a, b):
    return a.astype(jnp.float32) + b.astype(jnp.float32)


def chain_sum(pairs):
    held = [pairs[chain][3] for chain in range(2)]
    for k in (2, 1):
        got = [with_neighbour(held[chain], chain, (k + 1) % 2) for chain in range(2)]
        held = [add(got[chain], pairs[chain][k]).astype(jnp.bfloat16) for chain in range(2)]
    sums = []
    got = [with_neighbour(held[chain], chain, 1) for chain in range(2)]
    for chain in range(2):
        second = is_second(chain)
        give, keep = (
            add(jnp.where(second, x[0], x[1]), jnp.where(second, y[0], y[1]))
            for x, y in ((got[chain], pairs[chain][0]), (got[chain][::-1], pairs[chain][0][::-1]))
        )
        sums.append(keep + with_neighbour(give.astype(jnp.bfloat16), chain, 0).astype(jnp.float32))
    return jnp.concatenate(sums, axis=1)


def chain_gather(blocks):
    got = [with_neighbour(blocks[chain], chain, 0) for chain in range(2)]
    held = []
    for chain in range(2):
        second = is_second(chain)
        mine, other = blocks[chain], got[chain]
        held.append([jnp.stack([jnp.where(second, other, mine), jnp.where(second, mine, other)])])
    for k in range(1, 4):
        for chain in range(2):
            held[chain].append(with_neighbour(held[chain][-1], chain, k % 2))
    return held


def fold_kernel(wanted, started, me_ref, agg_ref, other_ref, *refs):
    grad_refs, out_ref = refs[started:-1], refs[-1]
    total = refs[0][...] if started else None
    for chain, rows_ref in enumerate((agg_ref, other_ref)):
        for i, k in enumerate(wanted):
            grads = grad_refs[len(wanted) * chain + i][...]
            rows = jnp.concatenate([rows_ref[pair_block(me_ref[0], chain, k, member)] for member in range(2)], axis=0)
            grads = grads.reshape(rows.shape[0], -1)
            term = lax.dot_general(rows, grads, (((0,), (0,)), ((), ())), preferred_element_type=jnp.float32)
            total = term if total is None else total + term
    out_ref[...] = total.astype(out_ref.dtype)


def fold(wanted, me, agg, other_agg, grads, start, kind):
    vmem = pl.BlockSpec(memory_space=pltpu.VMEM)
    grads = [*start, *(chain[k] for chain in grads for k in wanted)]
    return pl.pallas_call(
        functools.partial(fold_kernel, wanted, len(start)),
        out_shape=jax.ShapeDtypeStruct((agg.shape[2], grads[-1].shape[2]), kind),
        in_specs=[pl.BlockSpec(memory_space=pltpu.SMEM)] + [vmem] * (2 + len(grads)),
        out_specs=vmem,
        compiler_params=pltpu.CompilerParams(vmem_limit_bytes=16 * 2**20),
    )(me.reshape(1), agg, other_agg, *grads)


def shards(feature_table, sample_ids, block_ids, block_counts, block_tiles, weight, target):
    block_total, slot_total, block_rows, block_width = block_tiles.shape
    node_total = block_total * block_rows
    me = lax.axis_index("feat")
    with jax.named_scope("pick"):
        slices = lax.all_to_all(pick(feature_table, sample_ids, block_total), "feat", 0, 0)
    with jax.named_scope("aggregate"):
        agg, *far = aggregate(me, block_ids, block_counts, slices, block_tiles, weight)
        other_agg = lax.ppermute(agg, "core", SWAP)
        near = project((0, 1, 2), me, agg, weight)
        parts = [[*near[chain], far[chain]] for chain in range(2)]
    with jax.named_scope("preact"):
        preact, other_agg = lax.optimization_barrier((chain_sum(parts), other_agg))
    with jax.named_scope("grad"):
        sigmoid_part = jax.nn.sigmoid(preact)
        hidden = preact * sigmoid_part
        hidden_width = hidden.shape[1]
        scales = lax.rsqrt(jnp.mean(hidden * hidden, axis=1, keepdims=True) + 1e-05)
        embedding = (hidden * scales).astype(jnp.bfloat16)
        cotangent = (embedding.astype(jnp.float32) - target.astype(jnp.float32)) / node_total
        projected = jnp.sum(cotangent * hidden, axis=1, keepdims=True)
        grad_hidden = scales * cotangent - scales**3 / hidden_width * hidden * projected
        slope = sigmoid_part * (1.0 + preact * (1.0 - sigmoid_part))
        grad_pre = (grad_hidden * slope).astype(jnp.bfloat16)
    with jax.named_scope("swap"):
        half = hidden_width // 2
        first = lax.axis_index("core") == 0
        left, right = grad_pre[:, :half], grad_pre[:, half:]
        mine, other = jnp.where(first, left, right), lax.ppermute(jnp.where(first, right, left), "core", SWAP)
    with jax.named_scope("fold"):
        grads = chain_gather([mine, other])
        folded = fold((0, 1, 2), me, agg, other_agg, grads, [], jnp.float32)
        folded = fold((3,), me, agg, other_agg, grads, [folded], jnp.bfloat16)
    weight_grad = group_sum(folded)
    return (embedding, weight_grad)


def solution(mesh):
    fine = Mesh(mesh.devices.reshape(4, 3, 4, 2, 8), ALL)
    return jax.shard_map(
        shards,
        mesh=fine,
        in_specs=(
            P(ALL, None),
            P(ALL),
            P(GRP, None),
            P(GRP),
            P(GRP, None, None, None),
            P("feat", None),
            P(ALL, None),
        ),
        out_specs=(P(ALL, None), P("feat", None)),
        check_vma=False,
    )
```

```python
import functools

import jax
import jax.numpy as jnp
from jax import lax
from jax.experimental import pallas as pl
from jax.experimental.pallas import tpu as pltpu
from jax.sharding import Mesh, PartitionSpec as P

GRP = ("x", "zo", "zi", "core")
ALL = GRP + ("feat",)
SWAP = [(0, 1), (1, 0)]
FEAT = 8


def neighbours(chain, odd_step):
    first = (chain + odd_step) % 2
    pairs = [((i + first) % FEAT, (i + 1 + first) % FEAT) for i in range(0, FEAT, 2)]
    return pairs + [(j, i) for i, j in pairs]


def with_neighbour(block, chain, odd_step):
    return lax.ppermute(block, "feat", neighbours(chain, odd_step))


def is_second(chain):
    return (lax.axis_index("feat") + chain) % 2 == 1


def exchange_sum(parts, axis):
    got = lax.all_to_all(parts, axis, 0, 0)
    return jnp.sum(got.astype(jnp.float32), axis=0)


def group_sum(term):
    rows, cols = term.shape
    with jax.named_scope("sum_x_zi"):
        part = exchange_sum(term.reshape(16, rows // 16, cols), ("x", "zi"))
    with jax.named_scope("sum_z"):
        parts = lax.all_gather(part.astype(jnp.bfloat16), ("zo", "zi"), axis=0, tiled=True)
        parts = parts.reshape(3, rows // 4, cols).astype(jnp.float32)
        part = jnp.sum(parts, axis=0).astype(jnp.bfloat16)
    with jax.named_scope("gather_x"):
        part = lax.all_gather(part, "x", axis=0, tiled=True)
    with jax.named_scope("gather_core"):
        other = lax.ppermute(part, "core", SWAP)
        first = lax.axis_index("core") == 0
        return jnp.concatenate([jnp.where(first, part, other), jnp.where(first, other, part)], axis=1).astype(jnp.float32)


def pick_kernel(wanted_ref, table_ref, out_ref):
    slices, _, width = out_ref.shape
    wanted = wanted_ref[...].T.astype(table_ref.dtype)
    for j in range(slices):
        rows = jnp.dot(wanted, table_ref[:, j * width:(j + 1) * width], preferred_element_type=jnp.float32)
        out_ref[j] = rows.astype(out_ref.dtype)


def pick(table, ids, slices):
    vmem = pl.BlockSpec(memory_space=pltpu.VMEM)
    shape = (table.shape[0], ids.shape[0])
    wanted = (lax.broadcasted_iota(jnp.int32, shape, 0) == ids[None, :]).astype(jnp.float32)
    return pl.pallas_call(
        pick_kernel,
        out_shape=jax.ShapeDtypeStruct((slices, ids.shape[0], table.shape[1] // slices), table.dtype),
        in_specs=[vmem, vmem],
        out_specs=vmem,
        compiler_params=pltpu.CompilerParams(vmem_limit_bytes=16 * 2**20),
    )(wanted, table)


def pair_block(me, chain, k, member):
    rank = lax.rem(me + chain, FEAT)
    side = 2 * lax.rem(rank, 2) - 1
    pair = lax.div(rank, 2) + (0, side, -side, 2)[k] + FEAT // 2
    return lax.rem(2 * lax.rem(pair, FEAT // 2) + member + FEAT - chain, FEAT)


def mean_block(own, ids_ref, counts_ref, slices_ref, tiles_ref):
    width, slots = slices_ref.shape[2], tiles_ref.shape[1]
    lhs = [jnp.where(s < counts_ref[own], tiles_ref[own, s], jnp.zeros((), jnp.bfloat16)) for s in range(slots)]
    rhs = [slices_ref[ids_ref[own, s]] for s in range(slots)]
    lhs, rhs = jnp.concatenate(lhs, axis=1), jnp.concatenate(rhs, axis=0)
    summed = jnp.dot(lhs, rhs, preferred_element_type=jnp.float32)
    degree = jnp.dot(lhs, jnp.ones((lhs.shape[1], 128), jnp.bfloat16), preferred_element_type=jnp.float32)
    return (summed / jnp.concatenate([degree] * (width // 128), axis=1)).astype(jnp.bfloat16)


def far_kernel(me_ref, ids_ref, counts_ref, slices_ref, tiles_ref, weight_ref, *part_refs):
    for chain, part_ref in enumerate(part_refs):
        _, rows, cols = part_ref.shape
        blocks = [pair_block(me_ref[0], chain, 3, member) for member in range(2)]
        lhs = jnp.concatenate([mean_block(own, ids_ref, counts_ref, slices_ref, tiles_ref) for own in blocks], axis=0)
        parts = jnp.dot(lhs, weight_ref[:, chain * cols:(chain + 1) * cols], preferred_element_type=jnp.float32)
        part_ref[...] = parts.astype(jnp.bfloat16).reshape(2, rows, cols)


def near_kernel(me_ref, ids_ref, counts_ref, slices_ref, tiles_ref, weight_ref, agg_ref, *part_refs):
    for own in range(slices_ref.shape[0]):
        agg_ref[own] = mean_block(own, ids_ref, counts_ref, slices_ref, tiles_ref)
    project_kernel((0, 1, 2), me_ref, agg_ref, weight_ref, *part_refs)


def aggregate(me, ids, counts, slices, tiles, weight):
    vmem, smem = pl.BlockSpec(memory_space=pltpu.VMEM), pl.BlockSpec(memory_space=pltpu.SMEM)
    pair = jax.ShapeDtypeStruct((2, slices.shape[1], weight.shape[1] // 2), jnp.bfloat16)
    whole = jax.ShapeDtypeStruct(slices.shape, jnp.bfloat16)

    def call(kernel, out):
        return pl.pallas_call(
            kernel,
            out_shape=out,
            in_specs=[smem] * 3 + [vmem] * 3,
            out_specs=[vmem] * len(out),
            compiler_params=pltpu.CompilerParams(vmem_limit_bytes=16 * 2**20),
        )(me.reshape(1), ids, counts, slices, tiles, weight)

    far = call(far_kernel, [pair] * 2)
    agg, *near = call(near_kernel, [whole] + [pair] * 6)
    return agg, [[*near[3 * chain:3 * chain + 3], far[chain]] for chain in range(2)]


def project_kernel(wanted, me_ref, agg_ref, weight_ref, *part_refs):
    rows = agg_ref.shape[1]
    count = len(wanted)
    for chain in range(2):
        refs = part_refs[count * chain:count * (chain + 1)]
        cols = refs[0].shape[2]
        blocks = [pair_block(me_ref[0], chain, k, member) for k in wanted for member in range(2)]
        lhs = jnp.concatenate([agg_ref[block] for block in blocks], axis=0)
        parts = jnp.dot(lhs, weight_ref[:, chain * cols:(chain + 1) * cols], preferred_element_type=jnp.float32)
        parts = parts.astype(jnp.bfloat16)
        for i in range(2 * count):
            refs[i // 2][i % 2] = parts[i * rows:(i + 1) * rows]


def add(a, b):
    return a.astype(jnp.float32) + b.astype(jnp.float32)


def chain_sum(pairs):
    held = [pairs[chain][3] for chain in range(2)]
    for k in (2, 1):
        got = [with_neighbour(held[chain], chain, (k + 1) % 2) for chain in range(2)]
        held = [add(got[chain], pairs[chain][k]).astype(jnp.bfloat16) for chain in range(2)]
    sums = []
    got = [with_neighbour(held[chain], chain, 1) for chain in range(2)]
    for chain in range(2):
        second = is_second(chain)
        give, keep = (
            add(jnp.where(second, x[0], x[1]), jnp.where(second, y[0], y[1]))
            for x, y in ((got[chain], pairs[chain][0]), (got[chain][::-1], pairs[chain][0][::-1]))
        )
        sums.append(keep + with_neighbour(give.astype(jnp.bfloat16), chain, 0).astype(jnp.float32))
    return jnp.concatenate(sums, axis=1)


def chain_gather(blocks):
    got = [with_neighbour(blocks[chain], chain, 0) for chain in range(2)]
    held = []
    for chain in range(2):
        second = is_second(chain)
        mine, other = blocks[chain], got[chain]
        held.append([jnp.stack([jnp.where(second, other, mine), jnp.where(second, mine, other)])])
    for k in range(1, 4):
        for chain in range(2):
            held[chain].append(with_neighbour(held[chain][-1], chain, k % 2))
    return held


def fold_kernel(wanted, started, me_ref, agg_ref, other_ref, *refs):
    grad_refs, out_ref = refs[started:-1], refs[-1]
    total = refs[0][...] if started else None
    for chain, rows_ref in enumerate((agg_ref, other_ref)):
        for i, k in enumerate(wanted):
            grads = grad_refs[len(wanted) * chain + i][...]
            rows = jnp.concatenate([rows_ref[pair_block(me_ref[0], chain, k, member)] for member in range(2)], axis=0)
            grads = grads.reshape(rows.shape[0], -1)
            term = lax.dot_general(rows, grads, (((0,), (0,)), ((), ())), preferred_element_type=jnp.float32)
            total = term if total is None else total + term
    out_ref[...] = total.astype(out_ref.dtype)


def fold(wanted, me, agg, other_agg, grads, start, kind):
    vmem = pl.BlockSpec(memory_space=pltpu.VMEM)
    grads = [*start, *(chain[k] for chain in grads for k in wanted)]
    return pl.pallas_call(
        functools.partial(fold_kernel, wanted, len(start)),
        out_shape=jax.ShapeDtypeStruct((agg.shape[2], grads[-1].shape[2]), kind),
        in_specs=[pl.BlockSpec(memory_space=pltpu.SMEM)] + [vmem] * (2 + len(grads)),
        out_specs=vmem,
        compiler_params=pltpu.CompilerParams(vmem_limit_bytes=16 * 2**20),
    )(me.reshape(1), agg, other_agg, *grads)


def shards(feature_table, sample_ids, block_ids, block_counts, block_tiles, weight, target):
    block_total, slot_total, block_rows, block_width = block_tiles.shape
    node_total = block_total * block_rows
    me = lax.axis_index("feat")
    with jax.named_scope("pick"):
        slices = lax.all_to_all(pick(feature_table, sample_ids, block_total), "feat", 0, 0)
    with jax.named_scope("aggregate"):
        agg, parts = aggregate(me, block_ids, block_counts, slices, block_tiles, weight)
        other_agg = lax.ppermute(agg, "core", SWAP)
    with jax.named_scope("preact"):
        preact, other_agg = lax.optimization_barrier((chain_sum(parts), other_agg))
    with jax.named_scope("grad"):
        sigmoid_part = jax.nn.sigmoid(preact)
        hidden = preact * sigmoid_part
        hidden_width = hidden.shape[1]
        scales = lax.rsqrt(jnp.mean(hidden * hidden, axis=1, keepdims=True) + 1e-05)
        embedding = (hidden * scales).astype(jnp.bfloat16)
        cotangent = (embedding.astype(jnp.float32) - target.astype(jnp.float32)) / node_total
        projected = jnp.sum(cotangent * hidden, axis=1, keepdims=True)
        grad_hidden = scales * cotangent - scales**3 / hidden_width * hidden * projected
        slope = sigmoid_part * (1.0 + preact * (1.0 - sigmoid_part))
        grad_pre = (grad_hidden * slope).astype(jnp.bfloat16)
    with jax.named_scope("swap"):
        half = hidden_width // 2
        first = lax.axis_index("core") == 0
        left, right = grad_pre[:, :half], grad_pre[:, half:]
        mine, other = jnp.where(first, left, right), lax.ppermute(jnp.where(first, right, left), "core", SWAP)
    with jax.named_scope("fold"):
        grads = chain_gather([mine, other])
        folded = fold((0, 1, 2), me, agg, other_agg, grads, [], jnp.float32)
        folded = fold((3,), me, agg, other_agg, grads, [folded], jnp.bfloat16)
    weight_grad = group_sum(folded)
    return (embedding, weight_grad)


def solution(mesh):
    fine = Mesh(mesh.devices.reshape(4, 3, 4, 2, 8), ALL)
    return jax.shard_map(
        shards,
        mesh=fine,
        in_specs=(
            P(ALL, None),
            P(ALL),
            P(GRP, None),
            P(GRP),
            P(GRP, None, None, None),
            P("feat", None),
            P(ALL, None),
        ),
        out_specs=(P(ALL, None), P("feat", None)),
        check_vma=False,
    )
```

```python
import functools

import jax
import jax.numpy as jnp
from jax import lax
from jax.experimental import pallas as pl
from jax.experimental.pallas import tpu as pltpu
from jax.sharding import Mesh, PartitionSpec as P

GRP = ("x", "zo", "zi", "core")
ALL = GRP + ("feat",)
SWAP = [(0, 1), (1, 0)]
FEAT = 8


def neighbours(chain, odd_step):
    first = (chain + odd_step) % 2
    pairs = [((i + first) % FEAT, (i + 1 + first) % FEAT) for i in range(0, FEAT, 2)]
    return pairs + [(j, i) for i, j in pairs]


def with_neighbour(block, chain, odd_step):
    return lax.ppermute(block, "feat", neighbours(chain, odd_step))


def is_second(chain):
    return (lax.axis_index("feat") + chain) % 2 == 1


def exchange_sum(parts, axis):
    got = lax.all_to_all(parts, axis, 0, 0)
    return jnp.sum(got.astype(jnp.float32), axis=0)


def group_sum(term):
    rows, cols = term.shape
    with jax.named_scope("sum_x_zi"):
        part = exchange_sum(term.reshape(16, rows // 16, cols), ("x", "zi"))
    with jax.named_scope("sum_z"):
        parts = lax.all_gather(part.astype(jnp.bfloat16), ("zo", "zi"), axis=0, tiled=True)
        parts = parts.reshape(3, rows // 4, cols).astype(jnp.float32)
        part = jnp.sum(parts, axis=0).astype(jnp.bfloat16)
    with jax.named_scope("gather_x"):
        part = lax.all_gather(part, "x", axis=0, tiled=True)
    with jax.named_scope("gather_core"):
        other = lax.ppermute(part, "core", SWAP)
        first = lax.axis_index("core") == 0
        return jnp.concatenate([jnp.where(first, part, other), jnp.where(first, other, part)], axis=1).astype(jnp.float32)


def pick_kernel(wanted_ref, table_ref, out_ref):
    slices, _, width = out_ref.shape
    wanted = wanted_ref[...].T.astype(table_ref.dtype)
    for j in range(slices):
        rows = jnp.dot(wanted, table_ref[:, j * width:(j + 1) * width], preferred_element_type=jnp.float32)
        out_ref[j] = rows.astype(out_ref.dtype)


def pick(table, ids, slices):
    vmem = pl.BlockSpec(memory_space=pltpu.VMEM)
    shape = (table.shape[0], ids.shape[0])
    wanted = (lax.broadcasted_iota(jnp.int32, shape, 0) == ids[None, :]).astype(jnp.float32)
    return pl.pallas_call(
        pick_kernel,
        out_shape=jax.ShapeDtypeStruct((slices, ids.shape[0], table.shape[1] // slices), table.dtype),
        in_specs=[vmem, vmem],
        out_specs=vmem,
        compiler_params=pltpu.CompilerParams(vmem_limit_bytes=60 * 2**20),
    )(wanted, table)


def pair_block(me, chain, k, member):
    rank = lax.rem(me + chain, FEAT)
    side = 2 * lax.rem(rank, 2) - 1
    pair = lax.div(rank, 2) + (0, side, -side, 2)[k] + FEAT // 2
    return lax.rem(2 * lax.rem(pair, FEAT // 2) + member + FEAT - chain, FEAT)


def mean_block(own, ids_ref, counts_ref, slices_ref, tiles_ref):
    width, slots = slices_ref.shape[2], tiles_ref.shape[1]
    lhs = [jnp.where(s < counts_ref[own], tiles_ref[own, s], jnp.zeros((), jnp.bfloat16)) for s in range(slots)]
    rhs = [slices_ref[ids_ref[own, s]] for s in range(slots)]
    lhs, rhs = jnp.concatenate(lhs, axis=1), jnp.concatenate(rhs, axis=0)
    summed = jnp.dot(lhs, rhs, preferred_element_type=jnp.float32)
    degree = jnp.dot(lhs, jnp.ones((lhs.shape[1], 128), jnp.bfloat16), preferred_element_type=jnp.float32)
    return (summed / jnp.concatenate([degree] * (width // 128), axis=1)).astype(jnp.bfloat16)


def far_kernel(me_ref, ids_ref, counts_ref, slices_ref, tiles_ref, weight_ref, *part_refs):
    for chain, part_ref in enumerate(part_refs):
        _, rows, cols = part_ref.shape
        blocks = [pair_block(me_ref[0], chain, 3, member) for member in range(2)]
        lhs = jnp.concatenate([mean_block(own, ids_ref, counts_ref, slices_ref, tiles_ref) for own in blocks], axis=0)
        parts = jnp.dot(lhs, weight_ref[:, chain * cols:(chain + 1) * cols], preferred_element_type=jnp.float32)
        part_ref[...] = parts.astype(jnp.bfloat16).reshape(2, rows, cols)


def near_kernel(me_ref, ids_ref, counts_ref, slices_ref, tiles_ref, weight_ref, agg_ref, *part_refs):
    for own in range(slices_ref.shape[0]):
        agg_ref[own] = mean_block(own, ids_ref, counts_ref, slices_ref, tiles_ref)
    project_kernel((0, 1, 2), me_ref, agg_ref, weight_ref, *part_refs)


def aggregate(me, ids, counts, slices, tiles, weight):
    vmem, smem = pl.BlockSpec(memory_space=pltpu.VMEM), pl.BlockSpec(memory_space=pltpu.SMEM)
    pair = jax.ShapeDtypeStruct((2, slices.shape[1], weight.shape[1] // 2), jnp.bfloat16)
    whole = jax.ShapeDtypeStruct(slices.shape, jnp.bfloat16)

    def call(kernel, out):
        return pl.pallas_call(
            kernel,
            out_shape=out,
            in_specs=[smem] * 3 + [vmem] * 3,
            out_specs=[vmem] * len(out),
            compiler_params=pltpu.CompilerParams(vmem_limit_bytes=16 * 2**20),
        )(me.reshape(1), ids, counts, slices, tiles, weight)

    far = call(far_kernel, [pair] * 2)
    agg, *near = call(near_kernel, [whole] + [pair] * 6)
    return agg, [[*near[3 * chain:3 * chain + 3], far[chain]] for chain in range(2)]


def project_kernel(wanted, me_ref, agg_ref, weight_ref, *part_refs):
    rows = agg_ref.shape[1]
    count = len(wanted)
    for chain in range(2):
        refs = part_refs[count * chain:count * (chain + 1)]
        cols = refs[0].shape[2]
        blocks = [pair_block(me_ref[0], chain, k, member) for k in wanted for member in range(2)]
        lhs = jnp.concatenate([agg_ref[block] for block in blocks], axis=0)
        parts = jnp.dot(lhs, weight_ref[:, chain * cols:(chain + 1) * cols], preferred_element_type=jnp.float32)
        parts = parts.astype(jnp.bfloat16)
        for i in range(2 * count):
            refs[i // 2][i % 2] = parts[i * rows:(i + 1) * rows]


def add(a, b):
    return a.astype(jnp.float32) + b.astype(jnp.float32)


def chain_sum(pairs):
    held = [pairs[chain][3] for chain in range(2)]
    for k in (2, 1):
        got = [with_neighbour(held[chain], chain, (k + 1) % 2) for chain in range(2)]
        held = [add(got[chain], pairs[chain][k]).astype(jnp.bfloat16) for chain in range(2)]
    sums = []
    got = [with_neighbour(held[chain], chain, 1) for chain in range(2)]
    for chain in range(2):
        second = is_second(chain)
        give, keep = (
            add(jnp.where(second, x[0], x[1]), jnp.where(second, y[0], y[1]))
            for x, y in ((got[chain], pairs[chain][0]), (got[chain][::-1], pairs[chain][0][::-1]))
        )
        sums.append(keep + with_neighbour(give.astype(jnp.bfloat16), chain, 0).astype(jnp.float32))
    return jnp.concatenate(sums, axis=1)


def chain_gather(blocks):
    got = [with_neighbour(blocks[chain], chain, 0) for chain in range(2)]
    held = []
    for chain in range(2):
        second = is_second(chain)
        mine, other = blocks[chain], got[chain]
        held.append([jnp.stack([jnp.where(second, other, mine), jnp.where(second, mine, other)])])
    for k in range(1, 4):
        for chain in range(2):
            held[chain].append(with_neighbour(held[chain][-1], chain, k % 2))
    return held


def fold_kernel(wanted, started, me_ref, agg_ref, other_ref, *refs):
    grad_refs, out_ref = refs[started:-1], refs[-1]
    total = refs[0][...] if started else None
    for chain, rows_ref in enumerate((agg_ref, other_ref)):
        for i, k in enumerate(wanted):
            grads = grad_refs[len(wanted) * chain + i][...]
            rows = jnp.concatenate([rows_ref[pair_block(me_ref[0], chain, k, member)] for member in range(2)], axis=0)
            grads = grads.reshape(rows.shape[0], -1)
            term = lax.dot_general(rows, grads, (((0,), (0,)), ((), ())), preferred_element_type=jnp.float32)
            total = term if total is None else total + term
    out_ref[...] = total.astype(out_ref.dtype)


def fold(wanted, me, agg, other_agg, grads, start, kind):
    vmem = pl.BlockSpec(memory_space=pltpu.VMEM)
    grads = [*start, *(chain[k] for chain in grads for k in wanted)]
    return pl.pallas_call(
        functools.partial(fold_kernel, wanted, len(start)),
        out_shape=jax.ShapeDtypeStruct((agg.shape[2], grads[-1].shape[2]), kind),
        in_specs=[pl.BlockSpec(memory_space=pltpu.SMEM)] + [vmem] * (2 + len(grads)),
        out_specs=vmem,
        compiler_params=pltpu.CompilerParams(vmem_limit_bytes=16 * 2**20),
    )(me.reshape(1), agg, other_agg, *grads)


def shards(feature_table, sample_ids, block_ids, block_counts, block_tiles, weight, target):
    block_total, slot_total, block_rows, block_width = block_tiles.shape
    node_total = block_total * block_rows
    me = lax.axis_index("feat")
    with jax.named_scope("pick"):
        slices = lax.all_to_all(pick(feature_table, sample_ids, block_total), "feat", 0, 0)
    with jax.named_scope("aggregate"):
        agg, parts = aggregate(me, block_ids, block_counts, slices, block_tiles, weight)
        other_agg = lax.ppermute(agg, "core", SWAP)
    with jax.named_scope("preact"):
        preact, other_agg = lax.optimization_barrier((chain_sum(parts), other_agg))
    with jax.named_scope("grad"):
        sigmoid_part = jax.nn.sigmoid(preact)
        hidden = preact * sigmoid_part
        hidden_width = hidden.shape[1]
        scales = lax.rsqrt(jnp.mean(hidden * hidden, axis=1, keepdims=True) + 1e-05)
        embedding = (hidden * scales).astype(jnp.bfloat16)
        cotangent = (embedding.astype(jnp.float32) - target.astype(jnp.float32)) / node_total
        projected = jnp.sum(cotangent * hidden, axis=1, keepdims=True)
        grad_hidden = scales * cotangent - scales**3 / hidden_width * hidden * projected
        slope = sigmoid_part * (1.0 + preact * (1.0 - sigmoid_part))
        grad_pre = (grad_hidden * slope).astype(jnp.bfloat16)
    with jax.named_scope("swap"):
        half = hidden_width // 2
        first = lax.axis_index("core") == 0
        left, right = grad_pre[:, :half], grad_pre[:, half:]
        mine, other = jnp.where(first, left, right), lax.ppermute(jnp.where(first, right, left), "core", SWAP)
    with jax.named_scope("fold"):
        grads = chain_gather([mine, other])
        folded = fold((0, 1, 2), me, agg, other_agg, grads, [], jnp.float32)
        folded = fold((3,), me, agg, other_agg, grads, [folded], jnp.bfloat16)
    weight_grad = group_sum(folded)
    return (embedding, weight_grad)


def solution(mesh):
    fine = Mesh(mesh.devices.reshape(4, 3, 4, 2, 8), ALL)
    return jax.shard_map(
        shards,
        mesh=fine,
        in_specs=(
            P(ALL, None),
            P(ALL),
            P(GRP, None),
            P(GRP),
            P(GRP, None, None, None),
            P("feat", None),
            P(ALL, None),
        ),
        out_specs=(P(ALL, None), P("feat", None)),
        check_vma=False,
    )
```
